512 devices in a mesh: dp: 64 (over y_lo, z, core), fsdp: 8 (over x, y_hi).
Axes of the slice: x: 4, y: 4 (y_hi: 2, y_lo: 2; y = y_hi * 2 + y_lo), z: 16, core: 2. Of those that a mesh axis runs over, the one named last changes fastest.
Arguments:
- patches: bfloat16 [64, 8, 7, 64, 1280], P('dp', 'fsdp'), may hold values from -20 to 20
- norm_gain: float32 [1280], replicated, may hold values from 0.1 to 1.9
- w_qkv: bfloat16 [1280, 3840], P('fsdp'), may hold values from -0.5 to 0.5
- b_qkv: float32 [3840], replicated, may hold values from -3 to 3
- w_proj: bfloat16 [1280, 1280], P(None, 'fsdp'), may hold values from -0.15625 to 0.15625
- b_proj: float32 [1280], replicated, may hold values from -3 to 3
- merge_gain: float32 [1280], replicated, may hold values from 0.1 to 1.9
- groups: int32 [64, 8, 7], P(None, 'fsdp'), may hold values from 1 to 16
- route: int32 [64, 8, 7, 2], P(None, 'fsdp'), may hold values from -1 to 63, as said below
Outputs:
- merged: bfloat16 [64, 8, 4, 16, 5120], P('dp', 'fsdp')
The draws below stay inside these ranges and needn't reach their ends.
Inputs may be any that keep to these rules, and one draw needn't show every extreme that they name: In lane f, rank r keeps k_r windows (1 to 4) at slots 0 to k_r - 1 with route (r, j), and has s_r surplus windows (0 to 3) at slots 4 to 4 + s_r - 1; its k-th surplus slot 4 + k goes to rank (r + k + 1) mod 64 at a slot from k_(r + k + 1) to 3. All other slots hold -1, -1. Every owner rank of a lane receives exactly 4 windows, one at each owner slot 0 to 3; some rank of each lane has s_r = 3.
All inputs are finite; a program needn't handle non-finite values.
Results may differ from the reference program's by a relative error of at most 0.0055.
The reference program's roundings to bfloat16 on the way (of `placed`, `normed_in`, `projected`, `probability` and `attended`) count: a program that leaves them out, or rounds other values in their place, can miss the bound.
Values may be sent and summed in bfloat16 or wider, within the bound.
No kernel may reach another device: no remote copies, remote signals or barrier semaphores. Data moves between devices by JAX's collectives and lax.ppermute only.
A program may use at most 64 MiB of HBM per device.

```python
import math
import jax
import jax.numpy as jnp
from jax import lax

D = 1280
HEADS = 16
MERGE = 4
WIN = 64
RECV = 4
SLOTS = 7
N_DP = 64
N_FSDP = 8


def lane_plan(key):
    busy_key, extra_key, turn_key = jax.random.split(key, 3)
    ranks = jnp.arange(N_DP, dtype=jnp.int32)
    busy = jax.random.randint(busy_key, (N_DP,), 0, 2).astype(jnp.int32)
    extra = jax.random.randint(extra_key, (N_DP,), 1, RECV).astype(jnp.int32)
    surplus = busy * extra
    surplus = jnp.where(ranks >= N_DP - (RECV - 1), 0, surplus)
    surplus = surplus.at[0].set(RECV - 1)
    turn = jax.random.randint(turn_key, (), 0, N_DP).astype(jnp.int32)
    surplus = surplus[(ranks - turn) % N_DP]
    steps_ids = jnp.arange(RECV - 1, dtype=jnp.int32)
    senders = (ranks[:, None] - steps_ids[None, :] - 1) % N_DP
    incoming = (surplus[senders] > steps_ids[None, :]).astype(jnp.int32)
    kept = RECV - jnp.sum(incoming, axis=1)
    in_slot = kept[:, None] + jnp.cumsum(incoming, axis=1) - incoming
    slot_ids = jnp.arange(SLOTS, dtype=jnp.int32)
    own_live = slot_ids[None, :] < kept[:, None]
    moved_index = jnp.clip(slot_ids - RECV, 0, RECV - 2)
    moved_live = (slot_ids[None, :] >= RECV) & (slot_ids[None, :] < RECV + surplus[:, None])
    target = (ranks[:, None] + moved_index[None, :] + 1) % N_DP
    target_slot = in_slot[target, jnp.broadcast_to(moved_index[None, :], target.shape)]
    owner_rank = jnp.where(own_live, ranks[:, None], jnp.where(moved_live, target, -1))
    owner_slot = jnp.where(own_live, slot_ids[None, :], jnp.where(moved_live, target_slot, -1))
    return jnp.stack([owner_rank, owner_slot], axis=-1).astype(jnp.int32)


def draw_route(key, part):
    key = jax.random.fold_in(key, 41)
    plans = [lane_plan(jax.random.fold_in(key, lane_number)) for lane_number in range(N_FSDP)]
    return jnp.stack(plans, axis=1)


def draw_patches(key, part):
    key = jax.random.fold_in(key, 17)
    base_key, row_key, column_key = jax.random.split(key, 3)
    shape = (N_DP, N_FSDP, SLOTS, WIN, D)
    row_scale = jnp.exp(jax.random.uniform(row_key, (N_DP, N_FSDP, SLOTS, WIN, 1), jnp.float32, math.log(0.3), math.log(3.0)))
    column_scale = jnp.exp(jax.random.uniform(column_key, (D,), jnp.float32, math.log(0.3), math.log(3.0)))
    base = jnp.clip(jax.random.normal(base_key, shape, jnp.float32), -4.0, 4.0)
    return jnp.clip(base * row_scale * column_scale, -20.0, 20.0).astype(jnp.bfloat16)


def draw_w_qkv(key, part):
    key = jax.random.fold_in(key, 29)
    base_key = jax.random.fold_in(key, 0)
    base = jnp.clip(jax.random.normal(base_key, (D, 3 * D), jnp.float32), -4.0, 4.0) * D ** (-0.5)
    return jnp.clip(base, -0.5, 0.5).astype(jnp.bfloat16)


def set_ends(values, own_key, least, largest):
    spot = [jax.random.randint(jax.random.fold_in(own_key, axis), (), 0, length) for axis, length in enumerate(values.shape)]
    main_axis = values.shape.index(max(values.shape))
    neighbour = spot[:main_axis] + [(spot[main_axis] + 1) % values.shape[main_axis]] + spot[main_axis + 1:]
    return values.at[tuple(spot)].set(least).at[tuple(neighbour)].set(largest)


def shard_levels(rng, shape, pieces, smallest, largest):
    factor_of, own = 1.0, jax.random.fold_in(rng, 6)
    for axis_at, shards_of in pieces:
        steps = jnp.exp(jax.random.uniform(jax.random.fold_in(own, axis_at), (shards_of,), jnp.float32, smallest / len(pieces), largest / len(pieces)))
        factor_of = factor_of * jnp.repeat(steps, shape[axis_at] // shards_of).reshape([-1 if axis == axis_at else 1 for axis in range(len(shape))])
    return factor_of


def bell_draw(stream_key, dims, width, limit, cuts=(), kind=jnp.bfloat16):
    result = width * jax.random.normal(stream_key, dims, jnp.float32)
    if cuts:
        result = result * shard_levels(stream_key, dims, cuts, -0.22, 0.18)
    return jnp.clip(result, -limit, limit).astype(kind)


def setup_inputs(seed: int = 0) -> dict:
    arg_keys = jax.random.split(jax.random.key(seed), 10)
    patches = draw_patches(jax.random.fold_in(arg_keys[9], 71), 0)
    norm_gain = jnp.clip(1.0 + 0.18 * jax.random.normal(arg_keys[1], (D,), jnp.float32), 0.1, 1.9)
    w_qkv = draw_w_qkv(jax.random.fold_in(arg_keys[9], 71), 0)
    b_qkv = bell_draw(arg_keys[3], (3 * D,), 0.5, 3.0, (), jnp.float32)
    w_proj = bell_draw(arg_keys[4], (D, D), D ** -0.5, 0.15625, ((1, 8),))
    b_proj = bell_draw(arg_keys[5], (D,), 0.5, 3.0, (), jnp.float32)
    merge_gain = jnp.clip(1.0 + 0.18 * jax.random.normal(arg_keys[6], (D,), jnp.float32), 0.1, 1.9)
    groups = set_ends(jax.random.randint(arg_keys[7], (N_DP, N_FSDP, SLOTS), 1, WIN // MERGE + 1), jax.random.fold_in(arg_keys[7], 1), 1, (WIN // MERGE + 1) - 1).astype(jnp.int32)
    route = draw_route(jax.random.fold_in(arg_keys[9], 71), 0)
    return dict(patches=patches, norm_gain=norm_gain, w_qkv=w_qkv, b_qkv=b_qkv, w_proj=w_proj, b_proj=b_proj, merge_gain=merge_gain, groups=groups, route=route)


def encode(windows, group_counts, norm_gain, w_qkv, b_qkv, w_proj, b_proj, merge_gain):
    count_windows = windows.shape[0]
    head_size = D // HEADS
    whole = windows.astype(jnp.float32)
    normed_in = (whole * lax.rsqrt(lax.optimization_barrier(jnp.mean(whole * whole, axis=-1, keepdims=True)) + 1e-06) * norm_gain).astype(jnp.bfloat16)
    flat_rows = normed_in.reshape(count_windows * WIN, D)
    projected = (jnp.dot(flat_rows, w_qkv, preferred_element_type=jnp.float32) + b_qkv).astype(jnp.bfloat16)
    split_heads = projected.reshape(count_windows, WIN, 3, HEADS, head_size)
    queries = split_heads[:, :, 0].astype(jnp.float32)
    key_rows = split_heads[:, :, 1].astype(jnp.float32)
    values = split_heads[:, :, 2].astype(jnp.float32)
    scores = jnp.einsum('nqhd,nkhd->nhqk', queries, key_rows) * head_size ** (-0.5)
    live_keys = jnp.arange(WIN, dtype=jnp.int32)[None, :] < MERGE * group_counts[:, None]
    scores = jnp.where(live_keys[:, None, None, :], scores, -1e+30)
    row_top = lax.optimization_barrier(jnp.max(scores, axis=-1, keepdims=True))
    raised = jnp.exp(scores - row_top)
    probability = (raised / lax.optimization_barrier(jnp.sum(raised, axis=-1, keepdims=True))).astype(jnp.bfloat16)
    attended = jnp.einsum('nhqk,nkhd->nqhd', probability.astype(jnp.float32), values).astype(jnp.bfloat16)
    attended = attended.reshape(count_windows * WIN, D)
    residual = whole.reshape(count_windows * WIN, D) + jnp.dot(attended, w_proj, preferred_element_type=jnp.float32) + b_proj
    normed = residual * lax.rsqrt(lax.optimization_barrier(jnp.mean(residual * residual, axis=-1, keepdims=True)) + 1e-06) * merge_gain
    normed = normed.reshape(count_windows, WIN // MERGE, MERGE * D)
    kept_rows = jnp.arange(WIN // MERGE, dtype=jnp.int32)[None, :] < group_counts[:, None]
    return jnp.where(kept_rows[:, :, None], normed, 0.0).astype(jnp.bfloat16)

def reference(patches, norm_gain, w_qkv, b_qkv, w_proj, b_proj, merge_gain, groups, route):
    owner_rank = route[..., 0]
    owner_slot = route[..., 1]
    lane_ids = jnp.broadcast_to(jnp.arange(N_FSDP, dtype=jnp.int32)[None, :, None], owner_rank.shape)
    safe_rank = jnp.where(owner_rank >= 0, owner_rank, N_DP).astype(jnp.int32)
    safe_slot = jnp.where(owner_slot >= 0, owner_slot, 0).astype(jnp.int32)
    placed = jnp.zeros((N_DP, N_FSDP, RECV, WIN, D), patches.dtype).at[safe_rank, lane_ids, safe_slot].set(patches, mode='drop')
    placed_groups = jnp.zeros((N_DP, N_FSDP, RECV), jnp.int32).at[safe_rank, lane_ids, safe_slot].set(groups, mode='drop')
    flat_windows = placed.reshape(N_DP * N_FSDP, RECV, WIN, D)
    flat_groups = placed_groups.reshape(N_DP * N_FSDP, RECV)

    def one_owner(operands):
        return encode(operands[0], operands[1], norm_gain, w_qkv, b_qkv, w_proj, b_proj, merge_gain)
    merged = lax.map(one_owner, (flat_windows, flat_groups))
    return merged.reshape(N_DP, N_FSDP, RECV, WIN // MERGE, MERGE * D)
```

```python
import jax
import jax.numpy as jnp
from jax import lax
from jax.experimental import pallas as pl
from jax.experimental.pallas import tpu as pltpu
from jax.sharding import PartitionSpec as P

HEADS = 16
MERGE = 4
RECV = 4
SLOTS = 7
WIN = 64
D = 1280
HALF = D // 2
HEAD = D // HEADS
SHARDS = 8
DEPTH = D // SHARDS
ROWS = RECV * WIN
NX, NYH, NYL, NZ, NC = 4, 2, 2, 16, 2
AXES = ("dp", "fsdp")
EPS = 1e-06

NT = (((1,), (1,)), ((), ()))
TN = (((0,), (0,)), ((), ()))


def flat(x, yh, yl, z, c):
    return (((yl % NYL) * NZ + z % NZ) * NC + c) * SHARDS + (x % NX) * NYH + yh % NYH


def perm(move):
    places = [
        (x, yh, yl, z, c)
        for x in range(NX)
        for yh in range(NYH)
        for yl in range(NYL)
        for z in range(NZ)
        for c in range(NC)
    ]
    return [(flat(*p), flat(*move(*p))) for p in places]


def by_x(d):
    return perm(lambda x, yh, yl, z, c: (x + d, yh, yl, z, c))


def across_y():
    return perm(lambda x, yh, yl, z, c: (x, 1 - yh, 1 - yl, z, c))


def other_core():
    return perm(lambda x, yh, yl, z, c: (x, yh, yl, z, 1 - c))


def send(value, pairs):
    return lax.ppermute(value, AXES, pairs)


def by_rank(value, by):
    devices = lax.axis_size("dp")
    return lax.ppermute(value, "dp", [(i, (i + by) % devices) for i in range(devices)])


def place_kernel(meta, own, in0, in1, in2, gain, placed, normed):
    for t in range(RECV):
        src = meta[t]
        window = jnp.where(
            src < RECV,
            own[0, 0, t],
            jnp.where(src == RECV, in0[...], jnp.where(src == RECV + 1, in1[...], in2[...])),
        )
        placed[pl.ds(t * WIN, WIN), :] = window
        x = window.astype(jnp.float32)
        ms = jnp.mean(x * x, axis=-1, keepdims=True)
        normed[pl.ds(t * WIN, WIN), :] = (x * lax.rsqrt(ms + EPS) * gain[...]).astype(jnp.bfloat16)


def attend_kernel(meta, xa, xb, bias, *rest):
    pieces, (outa, outb, w, q, k, v, sems) = rest[:SHARDS], rest[SHARDS:]
    copies = []
    for i in range(SHARDS):
        at = pl.multiple_of(meta[12 + i] * DEPTH, DEPTH)
        copies.append(pltpu.make_async_copy(pieces[i], w.at[pl.ds(at, DEPTH), :], sems.at[i]))
    for copy in copies:
        copy.start()
    for copy in copies:
        copy.wait()
    for j, dst in enumerate((q, k, v)):
        cols = pl.ds(j * HALF, HALF)
        for i, src in enumerate((xa, xb)):
            dst[pl.ds(i * ROWS, ROWS), :] = (
                jnp.dot(src[...], w[:, cols], preferred_element_type=jnp.float32) + bias[:, cols]
            ).astype(jnp.bfloat16)
    pair = 2 * HEAD
    lane = lax.broadcasted_iota(jnp.int32, (1, 256), 1)
    key_at = lax.broadcasted_iota(jnp.int32, (WIN, 1), 0)
    for wnd in range(2 * RECV):
        rows = pl.ds(wnd * WIN, WIN)
        live = key_at < MERGE * meta[4 + wnd]
        out = outa if wnd < RECV else outb
        tiles = [None] * (HALF // 128)
        for i in range(HALF // pair):
            lo = i * pair // 128 * 128
            off = i * pair - lo
            first = (lane >= off) & (lane < off + HEAD)
            second = (lane >= off + HEAD) & (lane < off + pair)
            cols = pl.ds(lo, 256)
            qw = q[rows, cols]
            q2 = jnp.concatenate(
                [
                    qw * first.astype(jnp.float32).astype(jnp.bfloat16),
                    qw * second.astype(jnp.float32).astype(jnp.bfloat16),
                ],
                axis=0,
            )
            s = lax.dot_general(k[rows, cols], q2, NT, preferred_element_type=jnp.float32)
            s = jnp.where(live, s * HEAD ** (-0.5), -1e30)
            e = jnp.exp(s - jnp.max(s, axis=0, keepdims=True))
            p = (e / jnp.sum(e, axis=0, keepdims=True)).astype(jnp.bfloat16)
            o = lax.dot_general(p, v[rows, cols], TN, preferred_element_type=jnp.float32)
            o = jnp.where(first, o[:WIN], jnp.where(second, o[WIN:], 0.0))
            for n in range(2):
                part = o[:, n * 128 : (n + 1) * 128]
                tile = lo // 128 + n
                tiles[tile] = part if tiles[tile] is None else tiles[tile] + part
        at = pl.ds(wnd % RECV * WIN, WIN)
        for n, tile in enumerate(tiles):
            out[at, pl.ds(n * 128, 128)] = tile.astype(jnp.bfloat16)


def merge_kernel(meta, atta, attb, wa, wb, placed, bias, gain, out, y):
    update = lax.dot_general(atta[...], wa[...], NT, preferred_element_type=jnp.float32)
    update += lax.dot_general(attb[...], wb[...], NT, preferred_element_type=jnp.float32)
    r = placed[...].astype(jnp.float32) + update + bias[...]
    ms = jnp.mean(r * r, axis=-1, keepdims=True)
    normed = r * lax.rsqrt(ms + EPS) * gain[...]
    for n in range(D // 128):
        y[n] = normed[:, n * 128 : (n + 1) * 128]
    tokens = WIN // MERGE
    at = lax.broadcasted_iota(jnp.int32, (RECV * tokens, 1), 0)
    limit = jnp.full((RECV * tokens, 1), meta[4], jnp.int32)
    for t in range(1, RECV):
        limit = jnp.where(at >= t * tokens, meta[4 + t] + t * tokens, limit)
    live = at < limit
    for i in range(MERGE):
        for n in range(D // 128):
            part = y[n, pl.ds(i, RECV * tokens, stride=MERGE), :]
            out[:, pl.ds(i * D + n * 128, 128)] = jnp.where(live, part, 0.0).astype(jnp.bfloat16)


def vmem(n):
    return [pl.BlockSpec(memory_space=pltpu.VMEM)] * n


SMEM = pl.BlockSpec(memory_space=pltpu.SMEM)
PARAMS = pltpu.CompilerParams(vmem_limit_bytes=20 * 1024 * 1024)


def tables(route, groups, rank, x, yh):
    ranks = lax.axis_size("dp")
    who = jnp.stack([rank, rank ^ 1])
    slot = jnp.arange(SLOTS, dtype=jnp.int32)
    sender = jnp.where(slot < RECV, who[:, None], (who[:, None] - slot + RECV - 1) % ranks)
    hot = sender[:, :, None] == jnp.arange(ranks, dtype=jnp.int32)
    lane_route = jnp.transpose(route[:, 0], (1, 2, 0))
    lane_groups = jnp.transpose(groups[:, 0], (1, 0))
    there = jnp.sum(jnp.where(hot[:, :, None], lane_route, 0), axis=-1)
    count = jnp.sum(jnp.where(hot, lane_groups, 0), axis=-1)
    target = jnp.arange(RECV, dtype=jnp.int32)
    lands = (there[:, :, 0] == who[:, None])[:, :, None] & (there[:, :, 1][:, :, None] == target)
    src = jnp.sum(jnp.where(lands, slot[None, :, None], 0), axis=1)
    grp = jnp.sum(jnp.where(lands, count[:, :, None], 0), axis=1)
    steps = [(0, 0), (-1, 0), (1, 0), (0, 1), (2, 0), (-1, 1), (1, 1), (2, 1)]
    shard = jnp.stack([((x + dx) % NX) * NYH + (yh + dy) % NYH for dx, dy in steps])
    return jnp.concatenate([src[0], grp[0], grp[1], shard]).astype(jnp.int32)


def on_device(patches, norm_gain, w_qkv, b_qkv, w_proj, b_proj, merge_gain, groups, route):
    rank = lax.axis_index("dp")
    lane = lax.axis_index("fsdp")
    core = rank % NC
    half = core * HALF

    piece = jnp.concatenate(
        [lax.dynamic_slice_in_dim(w_qkv, j * D + half, HALF, 1) for j in range(3)], axis=1
    )
    bias = jnp.concatenate(
        [lax.dynamic_slice_in_dim(b_qkv, j * D + half, HALF, 0) for j in range(3)]
    )
    plus = send(piece, by_x(1))
    minus = send(piece, by_x(-1))
    cross = send(piece, across_y())
    far = send(piece, by_x(2))
    moved = []
    for m in range(SLOTS - RECV):
        window = patches[0, 0, RECV + m]
        if moved:
            window, moved[-1] = lax.optimization_barrier((window, moved[-1]))
        moved.append(by_rank(window, m + 1))

    w_out = lax.dynamic_slice_in_dim(jnp.transpose(w_proj), half, HALF, 1)
    plus, minus, cross, far, w_out, *moved = lax.optimization_barrier(
        (plus, minus, cross, far, w_out, *moved)
    )
    cross_plus = send(cross, by_x(1))
    cross_minus = send(cross, by_x(-1))
    cross_far = send(far, across_y())
    w_mine = lax.all_gather(w_out, "fsdp", axis=0, tiled=True)
    meta = tables(route, groups, rank, lane // NYH, lane % NYH)

    placed, normed = pl.pallas_call(
        place_kernel,
        out_shape=[jax.ShapeDtypeStruct((ROWS, D), jnp.bfloat16)] * 2,
        in_specs=[SMEM] + vmem(5),
        out_specs=vmem(2),
        compiler_params=PARAMS,
    )(meta, patches[:, :, :RECV], *moved, norm_gain.reshape(1, D))
    normed_other = send(normed, other_core())
    cross_plus, cross_minus, cross_far, w_mine, normed_other = lax.optimization_barrier(
        (cross_plus, cross_minus, cross_far, w_mine, normed_other)
    )
    w_other = send(w_mine, other_core())

    att, att_theirs = pl.pallas_call(
        attend_kernel,
        out_shape=[jax.ShapeDtypeStruct((ROWS, HALF), jnp.bfloat16)] * 2,
        in_specs=[SMEM] + vmem(3) + [pl.BlockSpec(memory_space=pltpu.HBM)] * SHARDS,
        out_specs=vmem(2),
        scratch_shapes=[pltpu.VMEM((D, 3 * HALF), jnp.bfloat16)]
        + [pltpu.VMEM((2 * ROWS, HALF), jnp.bfloat16)] * 3
        + [pltpu.SemaphoreType.DMA((SHARDS,))],
        compiler_params=PARAMS,
    )(
        meta, normed, normed_other, bias.reshape(1, 3 * HALF),
        piece, plus, minus, cross, far, cross_plus, cross_minus, cross_far,
    )
    att_other = send(att_theirs, other_core())

    merged = pl.pallas_call(
        merge_kernel,
        out_shape=jax.ShapeDtypeStruct((ROWS // MERGE, MERGE * D), jnp.bfloat16),
        in_specs=[SMEM] + vmem(7),
        out_specs=vmem(1)[0],
        scratch_shapes=[pltpu.VMEM((D // 128, ROWS, 128), jnp.float32)],
        compiler_params=PARAMS,
    )(
        meta, att, att_other, w_mine, w_other, placed,
        b_proj.reshape(1, D), merge_gain.reshape(1, D),
    )
    return merged.reshape(1, 1, RECV, WIN // MERGE, MERGE * D)


def solution(mesh):
    return jax.shard_map(
        on_device,
        mesh=mesh,
        in_specs=(
            P("dp", "fsdp", None, None, None),
            P(),
            P("fsdp", None),
            P(),
            P(None, "fsdp"),
            P(),
            P(),
            P(None, "fsdp", None),
            P(None, "fsdp", None, None),
        ),
        out_specs=P("dp", "fsdp", None, None, None),
        check_vma=False,
    )
```

```python
import jax
import jax.numpy as jnp
from jax import lax
from jax.experimental import pallas as pl
from jax.experimental.pallas import tpu as pltpu
from jax.sharding import PartitionSpec as P

HEADS = 16
MERGE = 4
RECV = 4
SLOTS = 7
WIN = 64
D = 1280
HALF = D // 2
HEAD = D // HEADS
SHARDS = 8
DEPTH = D // SHARDS
ROWS = RECV * WIN
NX, NYH, NYL, NZ, NC = 4, 2, 2, 16, 2
AXES = ("dp", "fsdp")
EPS = 1e-06

NT = (((1,), (1,)), ((), ()))
TN = (((0,), (0,)), ((), ()))


def flat(x, yh, yl, z, c):
    return (((yl % NYL) * NZ + z % NZ) * NC + c) * SHARDS + (x % NX) * NYH + yh % NYH


def perm(move):
    places = [
        (x, yh, yl, z, c)
        for x in range(NX)
        for yh in range(NYH)
        for yl in range(NYL)
        for z in range(NZ)
        for c in range(NC)
    ]
    return [(flat(*p), flat(*move(*p))) for p in places]


def by_x(d):
    return perm(lambda x, yh, yl, z, c: (x + d, yh, yl, z, c))


def across_y():
    return perm(lambda x, yh, yl, z, c: (x, 1 - yh, 1 - yl, z, c))


def other_core():
    return perm(lambda x, yh, yl, z, c: (x, yh, yl, z, 1 - c))


def send(value, pairs):
    return lax.ppermute(value, AXES, pairs)


def by_rank(value, by):
    devices = lax.axis_size("dp")
    return lax.ppermute(value, "dp", [(i, (i + by) % devices) for i in range(devices)])


def place_kernel(meta, own, in0, in1, in2, gain, placed, normed, sems):
    for t in range(RECV):
        rows = placed.at[pl.ds(t * WIN, WIN), :]
        kept = own.at[0, 0, t]
        for at, ref in enumerate((kept, in0, in1, in2)):
            here = meta[t] < RECV if at == 0 else meta[t] == RECV - 1 + at

            @pl.when(here)
            def _(ref=ref, rows=rows, t=t):
                pltpu.make_async_copy(ref, rows, sems.at[t]).start()

    for t in range(RECV):
        rows = pl.ds(t * WIN, WIN)
        pltpu.make_async_copy(own.at[0, 0, t], placed.at[rows, :], sems.at[t]).wait()
        x = placed[rows, :].astype(jnp.float32)
        ms = jnp.mean(x * x, axis=-1, keepdims=True)
        normed[rows, :] = (x * lax.rsqrt(ms + EPS) * gain[...]).astype(jnp.bfloat16)


def gather_kernel(meta, *rest):
    pieces, (_, w, wo, sems) = rest[:SHARDS], rest[SHARDS:]
    copies = []
    for i in range(SHARDS):
        at = pl.ds(pl.multiple_of(meta[12 + i] * DEPTH, DEPTH), DEPTH)
        for j, dst in enumerate((w, wo)):
            cols = pl.ds(j * 3 * HALF, (3 - 2 * j) * HALF)
            copies.append(
                pltpu.make_async_copy(pieces[i].at[:, cols], dst.at[at, :], sems.at[i, j])
            )
    for copy in copies:
        copy.start()
    for copy in copies:
        copy.wait()


def attend_kernel(meta, xa, xb, bias, w, outa, outb, q, k, v):
    for j, dst in enumerate((q, k, v)):
        cols = pl.ds(j * HALF, HALF)
        for i, src in enumerate((xa, xb)):
            dst[pl.ds(i * ROWS, ROWS), :] = (
                jnp.dot(src[...], w[:, cols], preferred_element_type=jnp.float32) + bias[:, cols]
            ).astype(jnp.bfloat16)
    pair = 2 * HEAD
    lane = lax.broadcasted_iota(jnp.int32, (1, 256), 1)
    key_at = lax.broadcasted_iota(jnp.int32, (WIN, 1), 0)
    for wnd in range(2 * RECV):
        rows = pl.ds(wnd * WIN, WIN)
        live = key_at < MERGE * meta[4 + wnd]
        out = outa if wnd < RECV else outb
        tiles = [None] * (HALF // 128)
        for i in range(HALF // pair):
            lo = i * pair // 128 * 128
            off = i * pair - lo
            first = (lane >= off) & (lane < off + HEAD)
            second = (lane >= off + HEAD) & (lane < off + pair)
            cols = pl.ds(lo, 256)
            qw = q[rows, cols]
            q2 = jnp.concatenate(
                [
                    qw * first.astype(jnp.float32).astype(jnp.bfloat16),
                    qw * second.astype(jnp.float32).astype(jnp.bfloat16),
                ],
                axis=0,
            )
            s = lax.dot_general(k[rows, cols], q2, NT, preferred_element_type=jnp.float32)
            s = jnp.where(live, s * HEAD ** (-0.5), -1e30)
            e = jnp.exp(s - jnp.max(s, axis=0, keepdims=True))
            p = (e / jnp.sum(e, axis=0, keepdims=True)).astype(jnp.bfloat16)
            o = lax.dot_general(p, v[rows, cols], TN, preferred_element_type=jnp.float32)
            o = jnp.where(first, o[:WIN], jnp.where(second, o[WIN:], 0.0))
            for n in range(2):
                part = o[:, n * 128 : (n + 1) * 128]
                tile = lo // 128 + n
                tiles[tile] = part if tiles[tile] is None else tiles[tile] + part
        at = pl.ds(wnd % RECV * WIN, WIN)
        for n, tile in enumerate(tiles):
            out[at, pl.ds(n * 128, 128)] = tile.astype(jnp.bfloat16)


def merge_kernel(meta, atta, attb, wa, wb, placed, bias, gain, out, y):
    update = lax.dot_general(atta[...], wa[...], NT, preferred_element_type=jnp.float32)
    update += lax.dot_general(attb[...], wb[...], NT, preferred_element_type=jnp.float32)
    r = placed[...].astype(jnp.float32) + update + bias[...]
    ms = jnp.mean(r * r, axis=-1, keepdims=True)
    normed = r * lax.rsqrt(ms + EPS) * gain[...]
    for n in range(D // 128):
        y[n] = normed[:, n * 128 : (n + 1) * 128]
    tokens = WIN // MERGE
    at = lax.broadcasted_iota(jnp.int32, (RECV * tokens, 1), 0)
    limit = jnp.full((RECV * tokens, 1), meta[4], jnp.int32)
    for t in range(1, RECV):
        limit = jnp.where(at >= t * tokens, meta[4 + t] + t * tokens, limit)
    live = at < limit
    for i in range(MERGE):
        for n in range(D // 128):
            part = y[n, pl.ds(i, RECV * tokens, stride=MERGE), :]
            out[:, pl.ds(i * D + n * 128, 128)] = jnp.where(live, part, 0.0).astype(jnp.bfloat16)


def vmem(n):
    return [pl.BlockSpec(memory_space=pltpu.VMEM)] * n


ANY = pl.BlockSpec(memory_space=pl.ANY)
SMALL = pltpu.CompilerParams(vmem_limit_bytes=4 * 1024 * 1024)
SMEM = pl.BlockSpec(memory_space=pltpu.SMEM)
PARAMS = pltpu.CompilerParams(vmem_limit_bytes=20 * 1024 * 1024)


def tables(route, groups, rank, x, yh):
    ranks = lax.axis_size("dp")
    who = jnp.stack([rank, rank ^ 1])
    slot = jnp.arange(SLOTS, dtype=jnp.int32)
    sender = jnp.where(slot < RECV, who[:, None], (who[:, None] - slot + RECV - 1) % ranks)
    hot = sender[:, :, None] == jnp.arange(ranks, dtype=jnp.int32)
    lane_route = jnp.transpose(route[:, 0], (1, 2, 0))
    lane_groups = jnp.transpose(groups[:, 0], (1, 0))
    there = jnp.sum(jnp.where(hot[:, :, None], lane_route, 0), axis=-1)
    count = jnp.sum(jnp.where(hot, lane_groups, 0), axis=-1)
    target = jnp.arange(RECV, dtype=jnp.int32)
    lands = (there[:, :, 0] == who[:, None])[:, :, None] & (there[:, :, 1][:, :, None] == target)
    src = jnp.sum(jnp.where(lands, slot[None, :, None], 0), axis=1)
    grp = jnp.sum(jnp.where(lands, count[:, :, None], 0), axis=1)
    steps = [(0, 0), (-1, 0), (1, 0), (0, 1), (2, 0), (-1, 1), (1, 1), (2, 1)]
    shard = jnp.stack([((x + dx) % NX) * NYH + (yh + dy) % NYH for dx, dy in steps])
    return jnp.concatenate([src[0], grp[0], grp[1], shard]).astype(jnp.int32)


def on_device(patches, norm_gain, w_qkv, b_qkv, w_proj, b_proj, merge_gain, groups, route):
    rank = lax.axis_index("dp")
    lane = lax.axis_index("fsdp")
    core = rank % NC
    half = core * HALF

    piece = jnp.concatenate(
        [lax.dynamic_slice_in_dim(w_qkv, j * D + half, HALF, 1) for j in range(3)]
        + [lax.dynamic_slice_in_dim(jnp.transpose(w_proj), half, HALF, 1)],
        axis=1,
    )
    bias = jnp.concatenate(
        [lax.dynamic_slice_in_dim(b_qkv, j * D + half, HALF, 0) for j in range(3)]
    )
    far = send(piece, by_x(2))
    cross = send(piece, across_y())
    plus = send(piece, by_x(1))
    minus = send(piece, by_x(-1))
    cross_plus = send(cross, by_x(1))
    cross_minus = send(cross, by_x(-1))
    cross_far = send(far, across_y())

    moved = [by_rank(patches[0, 0, RECV + m], m + 1) for m in range(SLOTS - RECV)]

    meta = tables(route, groups, rank, lane // NYH, lane % NYH)

    placed, normed = pl.pallas_call(
        place_kernel,
        out_shape=[jax.ShapeDtypeStruct((ROWS, D), jnp.bfloat16)] * 2,
        in_specs=[SMEM] + [ANY] * 4 + vmem(1),
        out_specs=vmem(2),
        scratch_shapes=[pltpu.SemaphoreType.DMA((RECV,))],
        compiler_params=SMALL,
    )(meta, patches, *moved, norm_gain.reshape(1, D))
    normed_other = send(normed, other_core())

    w, w_mine = pl.pallas_call(
        gather_kernel,
        out_shape=[
            jax.ShapeDtypeStruct((D, 3 * HALF), jnp.bfloat16),
            jax.ShapeDtypeStruct((D, HALF), jnp.bfloat16),
        ],
        in_specs=[SMEM] + [ANY] * (SHARDS + 1),
        out_specs=vmem(2),
        scratch_shapes=[pltpu.SemaphoreType.DMA((SHARDS, 2))],
        compiler_params=PARAMS,
    )(meta, piece, plus, minus, cross, far, cross_plus, cross_minus, cross_far, normed_other)
    w_other = send(w_mine, other_core())

    att, att_theirs = pl.pallas_call(
        attend_kernel,
        out_shape=[jax.ShapeDtypeStruct((ROWS, HALF), jnp.bfloat16)] * 2,
        in_specs=[SMEM] + vmem(4),
        out_specs=vmem(2),
        scratch_shapes=[pltpu.VMEM((2 * ROWS, HALF), jnp.bfloat16)] * 3,
        compiler_params=PARAMS,
    )(meta, normed, normed_other, bias.reshape(1, 3 * HALF), w)
    att_other = send(att_theirs, other_core())

    merged = pl.pallas_call(
        merge_kernel,
        out_shape=jax.ShapeDtypeStruct((ROWS // MERGE, MERGE * D), jnp.bfloat16),
        in_specs=[SMEM] + vmem(7),
        out_specs=vmem(1)[0],
        scratch_shapes=[pltpu.VMEM((D // 128, ROWS, 128), jnp.float32)],
        compiler_params=PARAMS,
    )(
        meta, att, att_other, w_mine, w_other, placed,
        b_proj.reshape(1, D), merge_gain.reshape(1, D),
    )
    return merged.reshape(1, 1, RECV, WIN // MERGE, MERGE * D)


def solution(mesh):
    return jax.shard_map(
        on_device,
        mesh=mesh,
        in_specs=(
            P("dp", "fsdp", None, None, None),
            P(),
            P("fsdp", None),
            P(),
            P(None, "fsdp"),
            P(),
            P(),
            P(None, "fsdp", None),
            P(None, "fsdp", None, None),
        ),
        out_specs=P("dp", "fsdp", None, None, None),
        check_vma=False,
    )
```

```python
import jax
import jax.numpy as jnp
from jax import lax
from jax.experimental import pallas as pl
from jax.experimental.pallas import tpu as pltpu
from jax.sharding import PartitionSpec as P

HEADS = 16
MERGE = 4
RECV = 4
SLOTS = 7
WIN = 64
D = 1280
HALF = D // 2
HEAD = D // HEADS
SHARDS = 8
DEPTH = D // SHARDS
PART = DEPTH // 2
ROWS = RECV * WIN
NX, NYH, NYL, NZ, NC = 4, 2, 2, 16, 2
AXES = ("dp", "fsdp")
EPS = 1e-06

NT = (((1,), (1,)), ((), ()))
TN = (((0,), (0,)), ((), ()))


def flat(x, yh, yl, z, c):
    return (((yl % NYL) * NZ + z % NZ) * NC + c) * SHARDS + (x % NX) * NYH + yh % NYH


def perm(move):
    places = [
        (x, yh, yl, z, c)
        for x in range(NX)
        for yh in range(NYH)
        for yl in range(NYL)
        for z in range(NZ)
        for c in range(NC)
    ]
    return [(flat(*p), flat(*move(*p))) for p in places]


def by_x(d):
    return perm(lambda x, yh, yl, z, c: (x + d, yh, yl, z, c))


def by_z(d):
    return perm(lambda x, yh, yl, z, c: (x, yh, yl, z + d, c))


def across_y():
    return perm(lambda x, yh, yl, z, c: (x, 1 - yh, 1 - yl, z, c))


def other_core():
    return perm(lambda x, yh, yl, z, c: (x, yh, yl, z, 1 - c))


def send(value, pairs):
    return lax.ppermute(value, AXES, pairs)


def by_rank(value, by):
    devices = lax.axis_size("dp")
    return lax.ppermute(value, "dp", [(i, (i + by) % devices) for i in range(devices)])


def place_kernel(meta, own, in0, in1, in2, gain, placed, normed, sems):
    for t in range(RECV):
        rows = placed.at[pl.ds(t * WIN, WIN), :]
        kept = own.at[0, 0, t]
        for at, ref in enumerate((kept, in0, in1, in2)):
            here = meta[t] < RECV if at == 0 else meta[t] == RECV - 1 + at

            @pl.when(here)
            def _(ref=ref, rows=rows, t=t):
                pltpu.make_async_copy(ref, rows, sems.at[t]).start()

    for t in range(RECV):
        rows = pl.ds(t * WIN, WIN)
        pltpu.make_async_copy(own.at[0, 0, t], placed.at[rows, :], sems.at[t]).wait()
        x = placed[rows, :].astype(jnp.float32)
        ms = jnp.mean(x * x, axis=-1, keepdims=True)
        normed[rows, :] = (x * lax.rsqrt(ms + EPS) * gain[...]).astype(jnp.bfloat16)


def spot(odd_half):
    rank = lax.axis_index("dp")
    half = pl.multiple_of(lax.rem(rank, NC) * HALF, 128)
    odd = lax.rem(lax.div(rank, NC), 2)
    return half, pl.multiple_of((1 - odd if odd_half else odd) * PART, PART)


def build_kernel(w, wo, *rest):
    out, sems = rest[-2:]
    half, row = spot(False)
    rows = pl.ds(0 if out.shape[0] == DEPTH else row, out.shape[0])
    copies = [
        pltpu.make_async_copy(
            w.at[rows, pl.ds(pl.multiple_of(half + j * D, 128), HALF)],
            out.at[:, pl.ds(j * HALF, HALF)],
            sems.at[j],
        )
        for j in range(3)
    ]
    copies.append(
        pltpu.make_async_copy(
            wo.at[rows, pl.ds(half, HALF)], out.at[:, pl.ds(3 * HALF, HALF)], sems.at[3]
        )
    )
    for copy in copies:
        copy.start()
    for copy in copies:
        copy.wait()


WHOLE = (0, 3, 4, 5, 6, 7)
HALVES = (1, 2)
PIECES = SHARDS + 2


def attend_kernel(meta, xa, xb, bias, *rest):
    mine, theirs, x, w, wo, q, k, v, att, x_sems, sems = rest[PIECES:]
    copies = [
        pltpu.make_async_copy(src, x.at[pl.ds(i * ROWS, ROWS), :], x_sems.at[i])
        for i, src in enumerate((xa, xb))
    ]
    for i, shard in enumerate((*WHOLE, *HALVES, *HALVES)):
        at = meta[12 + shard] * DEPTH
        if i >= len(WHOLE):
            at = at + spot(i >= SHARDS)[1]
        at = pl.ds(pl.multiple_of(at, PART), rest[i].shape[0])
        for j, dst in enumerate((w, wo)):
            cols = pl.ds(j * 3 * HALF, (3 - 2 * j) * HALF)
            copies.append(
                pltpu.make_async_copy(rest[i].at[:, cols], dst.at[at, :], sems.at[i, j])
            )
    for copy in copies:
        copy.start()
    for copy in copies:
        copy.wait()
    for j, dst in enumerate((q, k, v)):
        cols = pl.ds(j * HALF, HALF)
        for i in range(2):
            rows = pl.ds(i * ROWS, ROWS)
            dst[rows, :] = (
                jnp.dot(x[rows, :], w[:, cols], preferred_element_type=jnp.float32) + bias[:, cols]
            ).astype(jnp.bfloat16)
    pair = 2 * HEAD
    lane = lax.broadcasted_iota(jnp.int32, (1, 256), 1)
    key_at = lax.broadcasted_iota(jnp.int32, (WIN, 1), 0)
    for wnd in range(2 * RECV):
        rows = pl.ds(wnd * WIN, WIN)
        live = key_at < MERGE * meta[4 + wnd]
        tiles = [None] * (HALF // 128)
        for i in range(HALF // pair):
            lo = i * pair // 128 * 128
            off = i * pair - lo
            first = (lane >= off) & (lane < off + HEAD)
            second = (lane >= off + HEAD) & (lane < off + pair)
            cols = pl.ds(lo, 256)
            qw = q[rows, cols]
            q2 = jnp.concatenate(
                [
                    qw * first.astype(jnp.float32).astype(jnp.bfloat16),
                    qw * second.astype(jnp.float32).astype(jnp.bfloat16),
                ],
                axis=0,
            )
            s = lax.dot_general(k[rows, cols], q2, NT, preferred_element_type=jnp.float32)
            s = jnp.where(live, s * HEAD ** (-0.5), -1e30)
            e = jnp.exp(s - jnp.max(s, axis=0, keepdims=True))
            p = (e / jnp.sum(e, axis=0, keepdims=True)).astype(jnp.bfloat16)
            o = lax.dot_general(p, v[rows, cols], TN, preferred_element_type=jnp.float32)
            o = jnp.where(first, o[:WIN], jnp.where(second, o[WIN:], 0.0))
            for n in range(2):
                part = o[:, n * 128 : (n + 1) * 128]
                tile = lo // 128 + n
                tiles[tile] = part if tiles[tile] is None else tiles[tile] + part
        for n, tile in enumerate(tiles):
            att[rows, pl.ds(n * 128, 128)] = tile.astype(jnp.bfloat16)
    for i, out in enumerate((mine, theirs)):
        out[...] = lax.dot_general(
            att[pl.ds(i * ROWS, ROWS), :], wo[...], NT, preferred_element_type=jnp.float32
        )


def merge_kernel(meta, mine, other, placed, bias, gain, out, y):
    r = placed[...].astype(jnp.float32) + (mine[...] + other[...]) + bias[...]
    ms = jnp.mean(r * r, axis=-1, keepdims=True)
    normed = r * lax.rsqrt(ms + EPS) * gain[...]
    for n in range(D // 128):
        y[n] = normed[:, n * 128 : (n + 1) * 128]
    tokens = WIN // MERGE
    at = lax.broadcasted_iota(jnp.int32, (RECV * tokens, 1), 0)
    limit = jnp.full((RECV * tokens, 1), meta[4], jnp.int32)
    for t in range(1, RECV):
        limit = jnp.where(at >= t * tokens, meta[4 + t] + t * tokens, limit)
    live = at < limit
    for i in range(MERGE):
        for n in range(D // 128):
            part = y[n, pl.ds(i, RECV * tokens, stride=MERGE), :]
            out[:, pl.ds(i * D + n * 128, 128)] = jnp.where(live, part, 0.0).astype(jnp.bfloat16)


def build(rows, w, wo, *earlier):
    return pl.pallas_call(
        build_kernel,
        out_shape=jax.ShapeDtypeStruct((rows, 4 * HALF), jnp.bfloat16),
        in_specs=[ANY] * (2 + len(earlier)),
        out_specs=ANY,
        scratch_shapes=[pltpu.SemaphoreType.DMA((4,))],
        compiler_params=SMALL if earlier else LARGE,
    )(w, wo, *earlier)


def vmem(n):
    return [pl.BlockSpec(memory_space=pltpu.VMEM)] * n


ANY = pl.BlockSpec(memory_space=pl.ANY)
SMEM = pl.BlockSpec(memory_space=pltpu.SMEM)
SMALL = pltpu.CompilerParams(vmem_limit_bytes=4 * 1024 * 1024)
MIDDLE = pltpu.CompilerParams(vmem_limit_bytes=52 * 1024 * 1024)
LARGE = pltpu.CompilerParams(vmem_limit_bytes=60 * 1024 * 1024)
PARAMS = pltpu.CompilerParams(vmem_limit_bytes=24 * 1024 * 1024)


def tables(route, groups, rank, x, yh):
    ranks = lax.axis_size("dp")
    who = jnp.stack([rank, rank ^ 1])
    slot = jnp.arange(SLOTS, dtype=jnp.int32)
    sender = jnp.where(slot < RECV, who[:, None], (who[:, None] - slot + RECV - 1) % ranks)
    hot = sender[:, :, None] == jnp.arange(ranks, dtype=jnp.int32)
    lane_route = jnp.transpose(route[:, 0], (1, 2, 0))
    lane_groups = jnp.transpose(groups[:, 0], (1, 0))
    there = jnp.sum(jnp.where(hot[:, :, None], lane_route, 0), axis=-1)
    count = jnp.sum(jnp.where(hot, lane_groups, 0), axis=-1)
    target = jnp.arange(RECV, dtype=jnp.int32)
    lands = (there[:, :, 0] == who[:, None])[:, :, None] & (there[:, :, 1][:, :, None] == target)
    src = jnp.sum(jnp.where(lands, slot[None, :, None], 0), axis=1)
    grp = jnp.sum(jnp.where(lands, count[:, :, None], 0), axis=1)
    steps = [(0, 0), (-1, 0), (1, 0), (0, 1), (2, 0), (-1, 1), (1, 1), (2, 1)]
    shard = jnp.stack([((x + dx) % NX) * NYH + (yh + dy) % NYH for dx, dy in steps])
    return jnp.concatenate([src[0], grp[0], grp[1], shard]).astype(jnp.int32)


def on_device(patches, norm_gain, w_qkv, b_qkv, w_proj, b_proj, merge_gain, groups, route):
    rank = lax.axis_index("dp")
    lane = lax.axis_index("fsdp")
    core = rank % NC
    half = core * HALF

    w_out = jnp.transpose(w_proj)
    piece = build(DEPTH, w_qkv, w_out)
    bias = jnp.concatenate(
        [lax.dynamic_slice_in_dim(b_qkv, j * D + half, HALF, 0) for j in range(3)]
    )
    far = send(piece, by_x(2))
    cross = send(piece, across_y())
    moved = [by_rank(patches[0, 0, RECV + m], m + 1) for m in range(SLOTS - RECV)]
    part = build(PART, w_qkv, w_out, moved[0])
    plus = send(part, by_x(1))
    minus = send(part, by_x(-1))
    cross_plus = send(cross, by_x(1))
    cross_minus = send(cross, by_x(-1))
    cross_far = send(far, across_y())
    plus_rest = send(plus, by_z(1))
    minus_rest = send(minus, by_z(-1))

    meta = tables(route, groups, rank, lane // NYH, lane % NYH)

    placed, normed = pl.pallas_call(
        place_kernel,
        out_shape=[jax.ShapeDtypeStruct((ROWS, D), jnp.bfloat16)] * 2,
        in_specs=[SMEM] + [ANY] * 4 + vmem(1),
        out_specs=vmem(2),
        scratch_shapes=[pltpu.SemaphoreType.DMA((RECV,))],
        compiler_params=SMALL,
    )(meta, patches, *moved, norm_gain.reshape(1, D))
    normed_other = send(normed, other_core())

    mine, theirs = pl.pallas_call(
        attend_kernel,
        out_shape=[jax.ShapeDtypeStruct((ROWS, D), jnp.float32)] * 2,
        in_specs=[SMEM] + [ANY] * 2 + vmem(1) + [ANY] * PIECES,
        out_specs=vmem(2),
        scratch_shapes=[
            pltpu.VMEM((2 * ROWS, D), jnp.bfloat16),
            pltpu.VMEM((D, 3 * HALF), jnp.bfloat16),
            pltpu.VMEM((D, HALF), jnp.bfloat16),
        ]
        + [pltpu.VMEM((2 * ROWS, HALF), jnp.bfloat16)] * 4
        + [pltpu.SemaphoreType.DMA((2,)), pltpu.SemaphoreType.DMA((PIECES, 2))],
        compiler_params=MIDDLE,
    )(
        meta, normed, normed_other, bias.reshape(1, 3 * HALF),
        piece, cross, far, cross_plus, cross_minus, cross_far,
        plus, minus, plus_rest, minus_rest,
    )
    other = send(theirs, other_core())

    merged = pl.pallas_call(
        merge_kernel,
        out_shape=jax.ShapeDtypeStruct((ROWS // MERGE, MERGE * D), jnp.bfloat16),
        in_specs=[SMEM] + vmem(5),
        out_specs=vmem(1)[0],
        scratch_shapes=[pltpu.VMEM((D // 128, ROWS, 128), jnp.float32)],
        compiler_params=PARAMS,
    )(
        meta, mine, other, placed,
        b_proj.reshape(1, D), merge_gain.reshape(1, D),
    )
    return merged.reshape(1, 1, RECV, WIN // MERGE, MERGE * D)


def solution(mesh):
    return jax.shard_map(
        on_device,
        mesh=mesh,
        in_specs=(
            P("dp", "fsdp", None, None, None),
            P(),
            P("fsdp", None),
            P(),
            P(None, "fsdp"),
            P(),
            P(),
            P(None, "fsdp", None),
            P(None, "fsdp", None, None),
        ),
        out_specs=P("dp", "fsdp", None, None, None),
        check_vma=False,
    )
```

```python
import jax
import jax.numpy as jnp
from jax import lax
from jax.experimental import pallas as pl
from jax.experimental.pallas import tpu as pltpu
from jax.sharding import PartitionSpec as P

HEADS = 16
MERGE = 4
RECV = 4
SLOTS = 7
WIN = 64
D = 1280
HALF = D // 2
HEAD = D // HEADS
SHARDS = 8
DEPTH = D // SHARDS
ROWS = RECV * WIN
NX, NYH, NYL, NZ, NC = 4, 2, 2, 16, 2
AXES = ("dp", "fsdp")
EPS = 1e-06

NT = (((1,), (1,)), ((), ()))
TN = (((0,), (0,)), ((), ()))


def flat(x, yh, yl, z, c):
    return (((yl % NYL) * NZ + z % NZ) * NC + c) * SHARDS + (x % NX) * NYH + yh % NYH


def perm(move):
    places = [
        (x, yh, yl, z, c)
        for x in range(NX)
        for yh in range(NYH)
        for yl in range(NYL)
        for z in range(NZ)
        for c in range(NC)
    ]
    return [(flat(*p), flat(*move(*p))) for p in places]


def by_x(d):
    return perm(lambda x, yh, yl, z, c: (x + d, yh, yl, z, c))


def across_y():
    return perm(lambda x, yh, yl, z, c: (x, 1 - yh, 1 - yl, z, c))


def other_core():
    return perm(lambda x, yh, yl, z, c: (x, yh, yl, z, 1 - c))


def send(value, pairs):
    return lax.ppermute(value, AXES, pairs)


def by_rank(value, by):
    devices = lax.axis_size("dp")
    return lax.ppermute(value, "dp", [(i, (i + by) % devices) for i in range(devices)])


def place_kernel(meta, own, in0, in1, in2, gain, plus, minus, placed, normed, sems):
    for t in range(RECV):
        rows = placed.at[pl.ds(t * WIN, WIN), :]
        kept = own.at[0, 0, t]
        for at, ref in enumerate((kept, in0, in1, in2)):
            here = meta[t] < RECV if at == 0 else meta[t] == RECV - 1 + at

            @pl.when(here)
            def _(ref=ref, rows=rows, t=t):
                pltpu.make_async_copy(ref, rows, sems.at[t]).start()

    for t in range(RECV):
        rows = pl.ds(t * WIN, WIN)
        pltpu.make_async_copy(own.at[0, 0, t], placed.at[rows, :], sems.at[t]).wait()
        x = placed[rows, :].astype(jnp.float32)
        ms = jnp.mean(x * x, axis=-1, keepdims=True)
        normed[rows, :] = (x * lax.rsqrt(ms + EPS) * gain[...]).astype(jnp.bfloat16)


def gather_kernel(meta, *rest):
    pieces, (_, w, wo, sems) = rest[:SHARDS], rest[SHARDS:]
    copies = []
    for i in range(SHARDS):
        at = pl.ds(pl.multiple_of(meta[12 + i] * DEPTH, DEPTH), DEPTH)
        for j, dst in enumerate((w, wo)):
            cols = pl.ds(j * 3 * HALF, (3 - 2 * j) * HALF)
            copies.append(
                pltpu.make_async_copy(pieces[i].at[:, cols], dst.at[at, :], sems.at[i, j])
            )
    for copy in copies:
        copy.start()
    for copy in copies:
        copy.wait()


def attend_kernel(meta, xa, xb, bias, w, outa, outb, q, k, v):
    for j, dst in enumerate((q, k, v)):
        cols = pl.ds(j * HALF, HALF)
        for i, src in enumerate((xa, xb)):
            dst[pl.ds(i * ROWS, ROWS), :] = (
                jnp.dot(src[...], w[:, cols], preferred_element_type=jnp.float32) + bias[:, cols]
            ).astype(jnp.bfloat16)
    pair = 2 * HEAD
    lane = lax.broadcasted_iota(jnp.int32, (1, 256), 1)
    key_at = lax.broadcasted_iota(jnp.int32, (WIN, 1), 0)
    for wnd in range(2 * RECV):
        rows = pl.ds(wnd * WIN, WIN)
        live = key_at < MERGE * meta[4 + wnd]
        out = outa if wnd < RECV else outb
        tiles = [None] * (HALF // 128)
        for i in range(HALF // pair):
            lo = i * pair // 128 * 128
            off = i * pair - lo
            first = (lane >= off) & (lane < off + HEAD)
            second = (lane >= off + HEAD) & (lane < off + pair)
            cols = pl.ds(lo, 256)
            qw = q[rows, cols]
            q2 = jnp.concatenate(
                [
                    qw * first.astype(jnp.float32).astype(jnp.bfloat16),
                    qw * second.astype(jnp.float32).astype(jnp.bfloat16),
                ],
                axis=0,
            )
            s = lax.dot_general(k[rows, cols], q2, NT, preferred_element_type=jnp.float32)
            s = jnp.where(live, s * HEAD ** (-0.5), -1e30)
            e = jnp.exp(s - jnp.max(s, axis=0, keepdims=True))
            p = (e / jnp.sum(e, axis=0, keepdims=True)).astype(jnp.bfloat16)
            o = lax.dot_general(p, v[rows, cols], TN, preferred_element_type=jnp.float32)
            o = jnp.where(first, o[:WIN], jnp.where(second, o[WIN:], 0.0))
            for n in range(2):
                part = o[:, n * 128 : (n + 1) * 128]
                tile = lo // 128 + n
                tiles[tile] = part if tiles[tile] is None else tiles[tile] + part
        at = pl.ds(wnd % RECV * WIN, WIN)
        for n, tile in enumerate(tiles):
            out[at, pl.ds(n * 128, 128)] = tile.astype(jnp.bfloat16)


def merge_kernel(meta, atta, attb, wa, wb, placed, bias, gain, out, y):
    update = lax.dot_general(atta[...], wa[...], NT, preferred_element_type=jnp.float32)
    update += lax.dot_general(attb[...], wb[...], NT, preferred_element_type=jnp.float32)
    r = placed[...].astype(jnp.float32) + update + bias[...]
    ms = jnp.mean(r * r, axis=-1, keepdims=True)
    normed = r * lax.rsqrt(ms + EPS) * gain[...]
    for n in range(D // 128):
        y[n] = normed[:, n * 128 : (n + 1) * 128]
    tokens = WIN // MERGE
    at = lax.broadcasted_iota(jnp.int32, (RECV * tokens, 1), 0)
    limit = jnp.full((RECV * tokens, 1), meta[4], jnp.int32)
    for t in range(1, RECV):
        limit = jnp.where(at >= t * tokens, meta[4 + t] + t * tokens, limit)
    live = at < limit
    for i in range(MERGE):
        for n in range(D // 128):
            part = y[n, pl.ds(i, RECV * tokens, stride=MERGE), :]
            out[:, pl.ds(i * D + n * 128, 128)] = jnp.where(live, part, 0.0).astype(jnp.bfloat16)


def vmem(n):
    return [pl.BlockSpec(memory_space=pltpu.VMEM)] * n


ANY = pl.BlockSpec(memory_space=pl.ANY)
SMALL = pltpu.CompilerParams(vmem_limit_bytes=4 * 1024 * 1024)
SMEM = pl.BlockSpec(memory_space=pltpu.SMEM)
PARAMS = pltpu.CompilerParams(vmem_limit_bytes=20 * 1024 * 1024)


def tables(route, groups, rank, x, yh):
    ranks = lax.axis_size("dp")
    who = jnp.stack([rank, rank ^ 1])
    slot = jnp.arange(SLOTS, dtype=jnp.int32)
    sender = jnp.where(slot < RECV, who[:, None], (who[:, None] - slot + RECV - 1) % ranks)
    hot = sender[:, :, None] == jnp.arange(ranks, dtype=jnp.int32)
    lane_route = jnp.transpose(route[:, 0], (1, 2, 0))
    lane_groups = jnp.transpose(groups[:, 0], (1, 0))
    there = jnp.sum(jnp.where(hot[:, :, None], lane_route, 0), axis=-1)
    count = jnp.sum(jnp.where(hot, lane_groups, 0), axis=-1)
    target = jnp.arange(RECV, dtype=jnp.int32)
    lands = (there[:, :, 0] == who[:, None])[:, :, None] & (there[:, :, 1][:, :, None] == target)
    src = jnp.sum(jnp.where(lands, slot[None, :, None], 0), axis=1)
    grp = jnp.sum(jnp.where(lands, count[:, :, None], 0), axis=1)
    steps = [(0, 0), (-1, 0), (1, 0), (0, 1), (2, 0), (-1, 1), (1, 1), (2, 1)]
    shard = jnp.stack([((x + dx) % NX) * NYH + (yh + dy) % NYH for dx, dy in steps])
    return jnp.concatenate([src[0], grp[0], grp[1], shard]).astype(jnp.int32)


def on_device(patches, norm_gain, w_qkv, b_qkv, w_proj, b_proj, merge_gain, groups, route):
    rank = lax.axis_index("dp")
    lane = lax.axis_index("fsdp")
    core = rank % NC
    half = core * HALF

    piece = jnp.concatenate(
        [lax.dynamic_slice_in_dim(w_qkv, j * D + half, HALF, 1) for j in range(3)]
        + [lax.dynamic_slice_in_dim(jnp.transpose(w_proj), half, HALF, 1)],
        axis=1,
    )
    bias = jnp.concatenate(
        [lax.dynamic_slice_in_dim(b_qkv, j * D + half, HALF, 0) for j in range(3)]
    )
    moved = [by_rank(patches[0, 0, RECV + m], m + 1) for m in range(SLOTS - RECV)]
    piece, *moved = lax.optimization_barrier((piece, *moved))
    far = send(piece, by_x(2))
    cross = send(piece, across_y())
    plus = send(piece, by_x(1))
    minus = send(piece, by_x(-1))
    cross_plus = send(cross, by_x(1))
    cross_minus = send(cross, by_x(-1))
    cross_far = send(far, across_y())

    meta = tables(route, groups, rank, lane // NYH, lane % NYH)

    placed, normed = pl.pallas_call(
        place_kernel,
        out_shape=[jax.ShapeDtypeStruct((ROWS, D), jnp.bfloat16)] * 2,
        in_specs=[SMEM] + [ANY] * 4 + vmem(1) + [ANY] * 2,
        out_specs=vmem(2),
        scratch_shapes=[pltpu.SemaphoreType.DMA((RECV,))],
        compiler_params=SMALL,
    )(meta, patches, *moved, norm_gain.reshape(1, D), plus, minus)
    normed_other = send(normed, other_core())

    w, w_mine = pl.pallas_call(
        gather_kernel,
        out_shape=[
            jax.ShapeDtypeStruct((D, 3 * HALF), jnp.bfloat16),
            jax.ShapeDtypeStruct((D, HALF), jnp.bfloat16),
        ],
        in_specs=[SMEM] + [ANY] * (SHARDS + 1),
        out_specs=vmem(2),
        scratch_shapes=[pltpu.SemaphoreType.DMA((SHARDS, 2))],
        compiler_params=PARAMS,
    )(meta, piece, plus, minus, cross, far, cross_plus, cross_minus, cross_far, normed_other)
    w_other = send(w_mine, other_core())

    att, att_theirs = pl.pallas_call(
        attend_kernel,
        out_shape=[jax.ShapeDtypeStruct((ROWS, HALF), jnp.bfloat16)] * 2,
        in_specs=[SMEM] + vmem(4),
        out_specs=vmem(2),
        scratch_shapes=[pltpu.VMEM((2 * ROWS, HALF), jnp.bfloat16)] * 3,
        compiler_params=PARAMS,
    )(meta, normed, normed_other, bias.reshape(1, 3 * HALF), w)
    att_other = send(att_theirs, other_core())

    merged = pl.pallas_call(
        merge_kernel,
        out_shape=jax.ShapeDtypeStruct((ROWS // MERGE, MERGE * D), jnp.bfloat16),
        in_specs=[SMEM] + vmem(7),
        out_specs=vmem(1)[0],
        scratch_shapes=[pltpu.VMEM((D // 128, ROWS, 128), jnp.float32)],
        compiler_params=PARAMS,
    )(
        meta, att, att_other, w_mine, w_other, placed,
        b_proj.reshape(1, D), merge_gain.reshape(1, D),
    )
    return merged.reshape(1, 1, RECV, WIN // MERGE, MERGE * D)


def solution(mesh):
    return jax.shard_map(
        on_device,
        mesh=mesh,
        in_specs=(
            P("dp", "fsdp", None, None, None),
            P(),
            P("fsdp", None),
            P(),
            P(None, "fsdp"),
            P(),
            P(),
            P(None, "fsdp", None),
            P(None, "fsdp", None, None),
        ),
        out_specs=P("dp", "fsdp", None, None, None),
        check_vma=False,
    )
```

```python
import jax
import jax.numpy as jnp
from jax import lax
from jax.experimental import pallas as pl
from jax.experimental.pallas import tpu as pltpu
from jax.sharding import PartitionSpec as P

HEADS = 16
MERGE = 4
RECV = 4
SLOTS = 7
WIN = 64
D = 1280
HALF = D // 2
HEAD = D // HEADS
SHARDS = 8
DEPTH = D // SHARDS
ROWS = RECV * WIN
NX, NYH, NYL, NZ, NC = 4, 2, 2, 16, 2
AXES = ("dp", "fsdp")
EPS = 1e-06

NT = (((1,), (1,)), ((), ()))
TN = (((0,), (0,)), ((), ()))


def flat(x, yh, yl, z, c):
    return (((yl % NYL) * NZ + z % NZ) * NC + c) * SHARDS + (x % NX) * NYH + yh % NYH


def perm(move):
    places = [
        (x, yh, yl, z, c)
        for x in range(NX)
        for yh in range(NYH)
        for yl in range(NYL)
        for z in range(NZ)
        for c in range(NC)
    ]
    return [(flat(*p), flat(*move(*p))) for p in places]


def moves(even, odd=None):
    def move(x, yh, yl, z, c):
        dx, across = odd if c else even
        return x + dx, yh ^ across, yl ^ across, z, c

    pairs = perm(lambda *p: move(*p) if odd or p[-1] == 0 else p)
    return pairs if odd else [p for p in pairs if p[0] != p[1]]


def other_core():
    return perm(lambda x, yh, yl, z, c: (x, yh, yl, z, 1 - c))


def send(value, pairs):
    return lax.ppermute(value, AXES, pairs)


def by_rank(value, by):
    devices = lax.axis_size("dp")
    return lax.ppermute(value, "dp", [(i, (i + by) % devices) for i in range(devices)])


def place_kernel(meta, own, in0, in1, in2, gain, placed, normed, sems):
    for t in range(RECV):
        rows = placed.at[pl.ds(t * WIN, WIN), :]
        kept = own.at[0, 0, t]
        for at, ref in enumerate((kept, in0, in1, in2)):
            here = meta[t] < RECV if at == 0 else meta[t] == RECV - 1 + at

            @pl.when(here)
            def _(ref=ref, rows=rows, t=t):
                pltpu.make_async_copy(ref, rows, sems.at[t]).start()

    for t in range(RECV):
        rows = pl.ds(t * WIN, WIN)
        pltpu.make_async_copy(own.at[0, 0, t], placed.at[rows, :], sems.at[t]).wait()
        x = placed[rows, :].astype(jnp.float32)
        ms = jnp.mean(x * x, axis=-1, keepdims=True)
        normed[rows, :] = (x * lax.rsqrt(ms + EPS) * gain[...]).astype(jnp.bfloat16)


def gather_kernel(meta, own, a, b, c, d, early, late, _, w, wo, sems):
    core = lax.rem(lax.axis_index("dp"), NC)
    sources = [(ref, 0) for ref in (own, a, b, c)]
    sources += [(early, 0), (early, DEPTH), (late, 0)]

    def copies(i, ref, row):
        at = pl.multiple_of(meta[12 + i] * DEPTH, DEPTH)
        return [
            pltpu.make_async_copy(
                ref.at[pl.ds(row, DEPTH), pl.ds(j * 3 * HALF, (3 - 2 * j) * HALF)],
                dst.at[pl.ds(at, DEPTH), :],
                sems.at[i, j],
            )
            for j, dst in enumerate((w, wo))
        ]

    for i, source in enumerate(sources):
        for copy in copies(i, *source):
            copy.start()

    @pl.when(core == 0)
    def _():
        for copy in copies(SHARDS - 1, d, 0):
            copy.start()

    @pl.when(core != 0)
    def _():
        for copy in copies(SHARDS - 1, late, DEPTH):
            copy.start()

    for i, source in enumerate((*sources, (late, DEPTH))):
        for copy in copies(i, *source):
            copy.wait()


def attend_kernel(meta, xa, xb, bias, w, outa, outb, q, k, v):
    for j, dst in enumerate((q, k, v)):
        cols = pl.ds(j * HALF, HALF)
        for i, src in enumerate((xa, xb)):
            dst[pl.ds(i * ROWS, ROWS), :] = (
                jnp.dot(src[...], w[:, cols], preferred_element_type=jnp.float32) + bias[:, cols]
            ).astype(jnp.bfloat16)
    pair = 2 * HEAD
    lane = lax.broadcasted_iota(jnp.int32, (1, 256), 1)
    key_at = lax.broadcasted_iota(jnp.int32, (WIN, 1), 0)
    for wnd in range(2 * RECV):
        rows = pl.ds(wnd * WIN, WIN)
        live = key_at < MERGE * meta[4 + wnd]
        out = outa if wnd < RECV else outb
        tiles = [None] * (HALF // 128)
        for i in range(HALF // pair):
            lo = i * pair // 128 * 128
            off = i * pair - lo
            first = (lane >= off) & (lane < off + HEAD)
            second = (lane >= off + HEAD) & (lane < off + pair)
            cols = pl.ds(lo, 256)
            qw = q[rows, cols]
            q2 = jnp.concatenate(
                [
                    qw * first.astype(jnp.float32).astype(jnp.bfloat16),
                    qw * second.astype(jnp.float32).astype(jnp.bfloat16),
                ],
                axis=0,
            )
            s = lax.dot_general(k[rows, cols], q2, NT, preferred_element_type=jnp.float32)
            s = jnp.where(live, s * HEAD ** (-0.5), -1e30)
            e = jnp.exp(s - jnp.max(s, axis=0, keepdims=True))
            p = (e / jnp.sum(e, axis=0, keepdims=True)).astype(jnp.bfloat16)
            o = lax.dot_general(p, v[rows, cols], TN, preferred_element_type=jnp.float32)
            o = jnp.where(first, o[:WIN], jnp.where(second, o[WIN:], 0.0))
            for n in range(2):
                part = o[:, n * 128 : (n + 1) * 128]
                tile = lo // 128 + n
                tiles[tile] = part if tiles[tile] is None else tiles[tile] + part
        at = pl.ds(wnd % RECV * WIN, WIN)
        for n, tile in enumerate(tiles):
            out[at, pl.ds(n * 128, 128)] = tile.astype(jnp.bfloat16)


def merge_kernel(meta, atta, attb, wa, wb, placed, bias, gain, out, y):
    update = lax.dot_general(atta[...], wa[...], NT, preferred_element_type=jnp.float32)
    update += lax.dot_general(attb[...], wb[...], NT, preferred_element_type=jnp.float32)
    r = placed[...].astype(jnp.float32) + update + bias[...]
    ms = jnp.mean(r * r, axis=-1, keepdims=True)
    normed = r * lax.rsqrt(ms + EPS) * gain[...]
    for n in range(D // 128):
        y[n] = normed[:, n * 128 : (n + 1) * 128]
    tokens = WIN // MERGE
    at = lax.broadcasted_iota(jnp.int32, (RECV * tokens, 1), 0)
    limit = jnp.full((RECV * tokens, 1), meta[4], jnp.int32)
    for t in range(1, RECV):
        limit = jnp.where(at >= t * tokens, meta[4 + t] + t * tokens, limit)
    live = at < limit
    for i in range(MERGE):
        for n in range(D // 128):
            part = y[n, pl.ds(i, RECV * tokens, stride=MERGE), :]
            out[:, pl.ds(i * D + n * 128, 128)] = jnp.where(live, part, 0.0).astype(jnp.bfloat16)


def vmem(n):
    return [pl.BlockSpec(memory_space=pltpu.VMEM)] * n


ANY = pl.BlockSpec(memory_space=pl.ANY)
SMALL = pltpu.CompilerParams(vmem_limit_bytes=4 * 1024 * 1024)
SMEM = pl.BlockSpec(memory_space=pltpu.SMEM)
PARAMS = pltpu.CompilerParams(vmem_limit_bytes=20 * 1024 * 1024)


def tables(route, groups, rank, x, yh):
    ranks = lax.axis_size("dp")
    who = jnp.stack([rank, rank ^ 1])
    slot = jnp.arange(SLOTS, dtype=jnp.int32)
    sender = jnp.where(slot < RECV, who[:, None], (who[:, None] - slot + RECV - 1) % ranks)
    hot = sender[:, :, None] == jnp.arange(ranks, dtype=jnp.int32)
    lane_route = jnp.transpose(route[:, 0], (1, 2, 0))
    lane_groups = jnp.transpose(groups[:, 0], (1, 0))
    there = jnp.sum(jnp.where(hot[:, :, None], lane_route, 0), axis=-1)
    count = jnp.sum(jnp.where(hot, lane_groups, 0), axis=-1)
    target = jnp.arange(RECV, dtype=jnp.int32)
    lands = (there[:, :, 0] == who[:, None])[:, :, None] & (there[:, :, 1][:, :, None] == target)
    src = jnp.sum(jnp.where(lands, slot[None, :, None], 0), axis=1)
    grp = jnp.sum(jnp.where(lands, count[:, :, None], 0), axis=1)
    even = [(-1, 0), (0, 1), (-1, 1)]
    odd = [(1, 0), (2, 0), (2, 1)]
    orders = [
        [((x + dx) % NX) * NYH + (yh + dy) % NYH for dx, dy in [(0, 0), *one, *two, (1, 1)]]
        for one, two in ((even, odd), (odd, even))
    ]
    shard = jnp.where(rank % NC == 0, jnp.stack(orders[0]), jnp.stack(orders[1]))
    return jnp.concatenate([src[0], grp[0], grp[1], shard]).astype(jnp.int32)


def on_device(patches, norm_gain, w_qkv, b_qkv, w_proj, b_proj, merge_gain, groups, route):
    rank = lax.axis_index("dp")
    lane = lax.axis_index("fsdp")
    core = rank % NC
    half = core * HALF

    def columns(at):
        return jnp.concatenate(
            [lax.dynamic_slice_in_dim(w_qkv, j * D + at, HALF, 1) for j in range(3)]
            + [lax.dynamic_slice_in_dim(jnp.transpose(w_proj), at, HALF, 1)],
            axis=1,
        )

    piece = jnp.concatenate([columns(half), columns(HALF - half)], axis=0)
    bias = jnp.concatenate(
        [lax.dynamic_slice_in_dim(b_qkv, j * D + half, HALF, 0) for j in range(3)]
    )
    def halves_of(*shards):
        return jnp.concatenate([value[DEPTH:] for value in shards], axis=0)

    got_b = send(piece, moves((0, 1), (2, 0)))
    got_a = send(piece, moves((1, 0), (-1, 0)))
    got_c = send(got_b, moves((1, 0), (0, 1)))
    got_d = send(got_b, moves((-1, 0)))
    moved = [by_rank(patches[0, 0, RECV + m], m + 1) for m in range(SLOTS - RECV)]
    early, moved[0] = lax.optimization_barrier((halves_of(got_a, got_b), moved[0]))
    early = send(early, other_core())
    late = send(halves_of(got_c, got_d), other_core())


    meta = tables(route, groups, rank, lane // NYH, lane % NYH)

    placed, normed = pl.pallas_call(
        place_kernel,
        out_shape=[jax.ShapeDtypeStruct((ROWS, D), jnp.bfloat16)] * 2,
        in_specs=[SMEM] + [ANY] * 4 + vmem(1),
        out_specs=vmem(2),
        scratch_shapes=[pltpu.SemaphoreType.DMA((RECV,))],
        compiler_params=SMALL,
    )(meta, patches, *moved, norm_gain.reshape(1, D))
    normed_other = send(normed, other_core())

    w, w_mine = pl.pallas_call(
        gather_kernel,
        out_shape=[
            jax.ShapeDtypeStruct((D, 3 * HALF), jnp.bfloat16),
            jax.ShapeDtypeStruct((D, HALF), jnp.bfloat16),
        ],
        in_specs=[SMEM] + [ANY] * 8,
        out_specs=vmem(2),
        scratch_shapes=[pltpu.SemaphoreType.DMA((SHARDS, 2))],
        compiler_params=PARAMS,
    )(meta, piece, got_a, got_b, got_c, got_d, early, late, normed_other)
    w_other = send(w_mine, other_core())

    att, att_theirs = pl.pallas_call(
        attend_kernel,
        out_shape=[jax.ShapeDtypeStruct((ROWS, HALF), jnp.bfloat16)] * 2,
        in_specs=[SMEM] + vmem(4),
        out_specs=vmem(2),
        scratch_shapes=[pltpu.VMEM((2 * ROWS, HALF), jnp.bfloat16)] * 3,
        compiler_params=PARAMS,
    )(meta, normed, normed_other, bias.reshape(1, 3 * HALF), w)
    att_other = send(att_theirs, other_core())

    merged = pl.pallas_call(
        merge_kernel,
        out_shape=jax.ShapeDtypeStruct((ROWS // MERGE, MERGE * D), jnp.bfloat16),
        in_specs=[SMEM] + vmem(7),
        out_specs=vmem(1)[0],
        scratch_shapes=[pltpu.VMEM((D // 128, ROWS, 128), jnp.float32)],
        compiler_params=PARAMS,
    )(
        meta, att, att_other, w_mine, w_other, placed,
        b_proj.reshape(1, D), merge_gain.reshape(1, D),
    )
    return merged.reshape(1, 1, RECV, WIN // MERGE, MERGE * D)


def solution(mesh):
    return jax.shard_map(
        on_device,
        mesh=mesh,
        in_specs=(
            P("dp", "fsdp", None, None, None),
            P(),
            P("fsdp", None),
            P(),
            P(None, "fsdp"),
            P(),
            P(),
            P(None, "fsdp", None),
            P(None, "fsdp", None, None),
        ),
        out_specs=P("dp", "fsdp", None, None, None),
        check_vma=False,
    )
```

```python
import jax
import jax.numpy as jnp
from jax import lax
from jax.experimental import pallas as pl
from jax.experimental.pallas import tpu as pltpu
from jax.sharding import PartitionSpec as P

HEADS = 16
MERGE = 4
RECV = 4
SLOTS = 7
WIN = 64
D = 1280
HALF = D // 2
HEAD = D // HEADS
SHARDS = 8
DEPTH = D // SHARDS
ROWS = RECV * WIN
NX, NYH, NYL, NZ, NC = 4, 2, 2, 16, 2
AXES = ("dp", "fsdp")
EPS = 1e-06

NT = (((1,), (1,)), ((), ()))
TN = (((0,), (0,)), ((), ()))


def flat(x, yh, yl, z, c):
    return (((yl % NYL) * NZ + z % NZ) * NC + c) * SHARDS + (x % NX) * NYH + yh % NYH


def perm(move):
    places = [
        (x, yh, yl, z, c)
        for x in range(NX)
        for yh in range(NYH)
        for yl in range(NYL)
        for z in range(NZ)
        for c in range(NC)
    ]
    return [(flat(*p), flat(*move(*p))) for p in places]


def moves(even, odd=None):
    def move(x, yh, yl, z, c):
        dx, across = odd if c else even
        return x + dx, yh ^ across, yl ^ across, z, c

    pairs = perm(lambda *p: move(*p) if odd or p[-1] == 0 else p)
    return pairs if odd else [p for p in pairs if p[0] != p[1]]


def other_core():
    return perm(lambda x, yh, yl, z, c: (x, yh, yl, z, 1 - c))


def send(value, pairs):
    return lax.ppermute(value, AXES, pairs)


def by_rank(value, by):
    devices = lax.axis_size("dp")
    return lax.ppermute(value, "dp", [(i, (i + by) % devices) for i in range(devices)])


def place_kernel(meta, own, in0, in1, in2, gain, placed, normed, sems):
    for t in range(RECV):
        rows = placed.at[pl.ds(t * WIN, WIN), :]
        kept = own.at[0, 0, t]
        for at, ref in enumerate((kept, in0, in1, in2)):
            here = meta[t] < RECV if at == 0 else meta[t] == RECV - 1 + at

            @pl.when(here)
            def _(ref=ref, rows=rows, t=t):
                pltpu.make_async_copy(ref, rows, sems.at[t]).start()

    for t in range(RECV):
        rows = pl.ds(t * WIN, WIN)
        pltpu.make_async_copy(own.at[0, 0, t], placed.at[rows, :], sems.at[t]).wait()
        x = placed[rows, :].astype(jnp.float32)
        ms = jnp.mean(x * x, axis=-1, keepdims=True)
        normed[rows, :] = (x * lax.rsqrt(ms + EPS) * gain[...]).astype(jnp.bfloat16)


def gather_kernel(meta, own, a, b, c, d, early, late, _, w, wo, sems):
    core = lax.rem(lax.axis_index("dp"), NC)
    sources = [(ref, 0) for ref in (own, a, b, c)]
    sources += [(early, 0), (early, DEPTH), (late, 0)]

    def copies(i, ref, row):
        at = pl.multiple_of(meta[12 + i] * DEPTH, DEPTH)
        return [
            pltpu.make_async_copy(
                ref.at[pl.ds(row, DEPTH), pl.ds(j * 3 * HALF, (3 - 2 * j) * HALF)],
                dst.at[pl.ds(at, DEPTH), :],
                sems.at[i, j],
            )
            for j, dst in enumerate((w, wo))
        ]

    for i, source in enumerate(sources):
        for copy in copies(i, *source):
            copy.start()

    @pl.when(core == 0)
    def _():
        for copy in copies(SHARDS - 1, d, 0):
            copy.start()

    @pl.when(core != 0)
    def _():
        for copy in copies(SHARDS - 1, late, DEPTH):
            copy.start()

    for i, source in enumerate((*sources, (late, DEPTH))):
        for copy in copies(i, *source):
            copy.wait()


def attend_kernel(meta, xa, xb, bias, w, outa, outb, q, k, v):
    for j, dst in enumerate((q, k, v)):
        cols = pl.ds(j * HALF, HALF)
        for i, src in enumerate((xa, xb)):
            dst[pl.ds(i * ROWS, ROWS), :] = (
                jnp.dot(src[...], w[:, cols], preferred_element_type=jnp.float32) + bias[:, cols]
            ).astype(jnp.bfloat16)
    pair = 2 * HEAD
    lane = lax.broadcasted_iota(jnp.int32, (1, 256), 1)
    key_at = lax.broadcasted_iota(jnp.int32, (WIN, 1), 0)
    for wnd in range(2 * RECV):
        rows = pl.ds(wnd * WIN, WIN)
        live = key_at < MERGE * meta[4 + wnd]
        out = outa if wnd < RECV else outb
        tiles = [None] * (HALF // 128)
        for i in range(HALF // pair):
            lo = i * pair // 128 * 128
            off = i * pair - lo
            first = (lane >= off) & (lane < off + HEAD)
            second = (lane >= off + HEAD) & (lane < off + pair)
            cols = pl.ds(lo, 256)
            qw = q[rows, cols]
            q2 = jnp.concatenate(
                [
                    qw * first.astype(jnp.float32).astype(jnp.bfloat16),
                    qw * second.astype(jnp.float32).astype(jnp.bfloat16),
                ],
                axis=0,
            )
            s = lax.dot_general(k[rows, cols], q2, NT, preferred_element_type=jnp.float32)
            s = jnp.where(live, s * HEAD ** (-0.5), -1e30)
            e = jnp.exp(s - jnp.max(s, axis=0, keepdims=True))
            p = (e / jnp.sum(e, axis=0, keepdims=True)).astype(jnp.bfloat16)
            o = lax.dot_general(p, v[rows, cols], TN, preferred_element_type=jnp.float32)
            o = jnp.where(first, o[:WIN], jnp.where(second, o[WIN:], 0.0))
            for n in range(2):
                part = o[:, n * 128 : (n + 1) * 128]
                tile = lo // 128 + n
                tiles[tile] = part if tiles[tile] is None else tiles[tile] + part
        at = pl.ds(wnd % RECV * WIN, WIN)
        for n, tile in enumerate(tiles):
            out[at, pl.ds(n * 128, 128)] = tile.astype(jnp.bfloat16)


def merge_kernel(meta, atta, attb, wa, wb, placed, bias, gain, out, y):
    update = lax.dot_general(atta[...], wa[...], NT, preferred_element_type=jnp.float32)
    update += lax.dot_general(attb[...], wb[...], NT, preferred_element_type=jnp.float32)
    r = placed[...].astype(jnp.float32) + update + bias[...]
    ms = jnp.mean(r * r, axis=-1, keepdims=True)
    normed = r * lax.rsqrt(ms + EPS) * gain[...]
    for n in range(D // 128):
        y[n] = normed[:, n * 128 : (n + 1) * 128]
    tokens = WIN // MERGE
    at = lax.broadcasted_iota(jnp.int32, (RECV * tokens, 1), 0)
    limit = jnp.full((RECV * tokens, 1), meta[4], jnp.int32)
    for t in range(1, RECV):
        limit = jnp.where(at >= t * tokens, meta[4 + t] + t * tokens, limit)
    live = at < limit
    for i in range(MERGE):
        for n in range(D // 128):
            part = y[n, pl.ds(i, RECV * tokens, stride=MERGE), :]
            out[:, pl.ds(i * D + n * 128, 128)] = jnp.where(live, part, 0.0).astype(jnp.bfloat16)


def vmem(n):
    return [pl.BlockSpec(memory_space=pltpu.VMEM)] * n


ANY = pl.BlockSpec(memory_space=pl.ANY)
SMALL = pltpu.CompilerParams(vmem_limit_bytes=4 * 1024 * 1024)
SMEM = pl.BlockSpec(memory_space=pltpu.SMEM)
PARAMS = pltpu.CompilerParams(vmem_limit_bytes=20 * 1024 * 1024)


def tables(route, groups, rank, x, yh):
    ranks = lax.axis_size("dp")
    who = jnp.stack([rank, rank ^ 1])
    slot = jnp.arange(SLOTS, dtype=jnp.int32)
    sender = jnp.where(slot < RECV, who[:, None], (who[:, None] - slot + RECV - 1) % ranks)
    hot = sender[:, :, None] == jnp.arange(ranks, dtype=jnp.int32)
    lane_route = jnp.transpose(route[:, 0], (1, 2, 0))
    lane_groups = jnp.transpose(groups[:, 0], (1, 0))
    there = jnp.sum(jnp.where(hot[:, :, None], lane_route, 0), axis=-1)
    count = jnp.sum(jnp.where(hot, lane_groups, 0), axis=-1)
    target = jnp.arange(RECV, dtype=jnp.int32)
    lands = (there[:, :, 0] == who[:, None])[:, :, None] & (there[:, :, 1][:, :, None] == target)
    src = jnp.sum(jnp.where(lands, slot[None, :, None], 0), axis=1)
    grp = jnp.sum(jnp.where(lands, count[:, :, None], 0), axis=1)
    even = [(-1, 0), (0, 1), (-1, 1)]
    odd = [(1, 0), (2, 0), (2, 1)]
    orders = [
        [((x + dx) % NX) * NYH + (yh + dy) % NYH for dx, dy in [(0, 0), *one, *two, (1, 1)]]
        for one, two in ((even, odd), (odd, even))
    ]
    shard = jnp.where(rank % NC == 0, jnp.stack(orders[0]), jnp.stack(orders[1]))
    return jnp.concatenate([src[0], grp[0], grp[1], shard]).astype(jnp.int32)


def on_device(patches, norm_gain, w_qkv, b_qkv, w_proj, b_proj, merge_gain, groups, route):
    rank = lax.axis_index("dp")
    lane = lax.axis_index("fsdp")
    core = rank % NC
    half = core * HALF

    def columns(at):
        return jnp.concatenate(
            [lax.dynamic_slice_in_dim(w_qkv, j * D + at, HALF, 1) for j in range(3)]
            + [lax.dynamic_slice_in_dim(jnp.transpose(w_proj), at, HALF, 1)],
            axis=1,
        )

    piece = jnp.concatenate(
        lax.optimization_barrier([columns(half), columns(HALF - half)]), axis=0
    )
    bias = jnp.concatenate(
        [lax.dynamic_slice_in_dim(b_qkv, j * D + half, HALF, 0) for j in range(3)]
    )
    def halves_of(*shards):
        return jnp.concatenate([value[DEPTH:] for value in shards], axis=0)

    got_b = send(piece, moves((0, 1), (2, 0)))
    got_a = send(piece, moves((1, 0), (-1, 0)))
    moved = [by_rank(patches[0, 0, RECV + m], m + 1) for m in range(SLOTS - RECV)]
    got_b, *moved = lax.optimization_barrier((got_b, *moved))
    got_c = send(got_b, moves((1, 0), (0, 1)))
    got_d = send(got_b, moves((-1, 0)))
    early = send(halves_of(got_a, got_b), other_core())


    meta = tables(route, groups, rank, lane // NYH, lane % NYH)

    placed, normed = pl.pallas_call(
        place_kernel,
        out_shape=[jax.ShapeDtypeStruct((ROWS, D), jnp.bfloat16)] * 2,
        in_specs=[SMEM] + [ANY] * 4 + vmem(1),
        out_specs=vmem(2),
        scratch_shapes=[pltpu.SemaphoreType.DMA((RECV,))],
        compiler_params=SMALL,
    )(meta, patches, *moved, norm_gain.reshape(1, D))
    normed_other = send(normed, other_core())
    late, normed_other = lax.optimization_barrier((halves_of(got_c, got_d), normed_other))
    late = send(late, other_core())

    w, w_mine = pl.pallas_call(
        gather_kernel,
        out_shape=[
            jax.ShapeDtypeStruct((D, 3 * HALF), jnp.bfloat16),
            jax.ShapeDtypeStruct((D, HALF), jnp.bfloat16),
        ],
        in_specs=[SMEM] + [ANY] * 8,
        out_specs=vmem(2),
        scratch_shapes=[pltpu.SemaphoreType.DMA((SHARDS, 2))],
        compiler_params=PARAMS,
    )(meta, piece, got_a, got_b, got_c, got_d, early, late, normed_other)
    w_other = send(w_mine, other_core())

    att, att_theirs = pl.pallas_call(
        attend_kernel,
        out_shape=[jax.ShapeDtypeStruct((ROWS, HALF), jnp.bfloat16)] * 2,
        in_specs=[SMEM] + vmem(4),
        out_specs=vmem(2),
        scratch_shapes=[pltpu.VMEM((2 * ROWS, HALF), jnp.bfloat16)] * 3,
        compiler_params=PARAMS,
    )(meta, normed, normed_other, bias.reshape(1, 3 * HALF), w)
    att_other = send(att_theirs, other_core())

    merged = pl.pallas_call(
        merge_kernel,
        out_shape=jax.ShapeDtypeStruct((ROWS // MERGE, MERGE * D), jnp.bfloat16),
        in_specs=[SMEM] + vmem(7),
        out_specs=vmem(1)[0],
        scratch_shapes=[pltpu.VMEM((D // 128, ROWS, 128), jnp.float32)],
        compiler_params=PARAMS,
    )(
        meta, att, att_other, w_mine, w_other, placed,
        b_proj.reshape(1, D), merge_gain.reshape(1, D),
    )
    return merged.reshape(1, 1, RECV, WIN // MERGE, MERGE * D)


def solution(mesh):
    return jax.shard_map(
        on_device,
        mesh=mesh,
        in_specs=(
            P("dp", "fsdp", None, None, None),
            P(),
            P("fsdp", None),
            P(),
            P(None, "fsdp"),
            P(),
            P(),
            P(None, "fsdp", None),
            P(None, "fsdp", None, None),
        ),
        out_specs=P("dp", "fsdp", None, None, None),
        check_vma=False,
    )
```

```python
import jax
import jax.numpy as jnp
from jax import lax
from jax.experimental import pallas as pl
from jax.experimental.pallas import tpu as pltpu
from jax.sharding import PartitionSpec as P

HEADS = 16
MERGE = 4
RECV = 4
SLOTS = 7
WIN = 64
D = 1280
HALF = D // 2
HEAD = D // HEADS
SHARDS = 8
DEPTH = D // SHARDS
PART = DEPTH // 2
ROWS = RECV * WIN
NX, NYH, NYL, NZ, NC = 4, 2, 2, 16, 2
AXES = ("dp", "fsdp")
EPS = 1e-06

NT = (((1,), (1,)), ((), ()))
TN = (((0,), (0,)), ((), ()))


def flat(x, yh, yl, z, c):
    return (((yl % NYL) * NZ + z % NZ) * NC + c) * SHARDS + (x % NX) * NYH + yh % NYH


def perm(move):
    places = [
        (x, yh, yl, z, c)
        for x in range(NX)
        for yh in range(NYH)
        for yl in range(NYL)
        for z in range(NZ)
        for c in range(NC)
    ]
    return [(flat(*p), flat(*move(*p))) for p in places]


def moves(even, odd=None):
    def move(x, yh, yl, z, c):
        dx, across = odd if c else even
        return x + dx, yh ^ across, yl ^ across, z, c

    pairs = perm(lambda *p: move(*p) if odd or p[-1] == 0 else p)
    return pairs if odd else [p for p in pairs if p[0] != p[1]]


def planes():
    return perm(lambda x, yh, yl, z, c: (x, yh, yl, z - 1 if c else z + 1, c))


def other_core():
    return perm(lambda x, yh, yl, z, c: (x, yh, yl, z, 1 - c))


def send(value, pairs):
    return lax.ppermute(value, AXES, pairs)


def by_rank(value, by):
    devices = lax.axis_size("dp")
    return lax.ppermute(value, "dp", [(i, (i + by) % devices) for i in range(devices)])


def place_kernel(meta, own, in0, in1, in2, gain, placed, normed, sems):
    for t in range(RECV):
        rows = placed.at[pl.ds(t * WIN, WIN), :]
        kept = own.at[0, 0, t]
        for at, ref in enumerate((kept, in0, in1, in2)):
            here = meta[t] < RECV if at == 0 else meta[t] == RECV - 1 + at

            @pl.when(here)
            def _(ref=ref, rows=rows, t=t):
                pltpu.make_async_copy(ref, rows, sems.at[t]).start()

    for t in range(RECV):
        rows = pl.ds(t * WIN, WIN)
        pltpu.make_async_copy(own.at[0, 0, t], placed.at[rows, :], sems.at[t]).wait()
        x = placed[rows, :].astype(jnp.float32)
        ms = jnp.mean(x * x, axis=-1, keepdims=True)
        normed[rows, :] = (x * lax.rsqrt(ms + EPS) * gain[...]).astype(jnp.bfloat16)


def gather_kernel(meta, own, a, b, c, d, rest_a, early, late, _, w, wo, sems):
    core = lax.rem(lax.axis_index("dp"), NC)
    near = lax.rem(lax.div(lax.axis_index("dp"), NC), 2) * PART
    away = PART - near
    sources = [
        (0, own, 0, DEPTH, 0),
        (1, a, 0, PART, near),
        (1, rest_a, 0, PART, away),
        (2, b, 0, DEPTH, 0),
        (3, c, 0, DEPTH, 0),
        (4, early, 0, PART, near),
        (4, early, PART, PART, away),
        (5, early, DEPTH, DEPTH, 0),
        (6, late, 0, DEPTH, 0),
    ]
    last = len(sources)

    def copies(i, shard, ref, row, rows, to):
        at = pl.multiple_of(meta[12 + shard] * DEPTH + to, PART)
        return [
            pltpu.make_async_copy(
                ref.at[pl.ds(row, rows), pl.ds(j * 3 * HALF, (3 - 2 * j) * HALF)],
                dst.at[pl.ds(at, rows), :],
                sems.at[i, j],
            )
            for j, dst in enumerate((w, wo))
        ]

    for i, source in enumerate(sources):
        for copy in copies(i, *source):
            copy.start()

    @pl.when(core == 0)
    def _():
        for copy in copies(last, SHARDS - 1, d, 0, DEPTH, 0):
            copy.start()

    @pl.when(core != 0)
    def _():
        for copy in copies(last, SHARDS - 1, late, DEPTH, DEPTH, 0):
            copy.start()

    for i, source in enumerate((*sources, (SHARDS - 1, late, DEPTH, DEPTH, 0))):
        for copy in copies(i, *source):
            copy.wait()


def attend_kernel(meta, xa, xb, bias, w, outa, outb, q, k, v):
    for j, dst in enumerate((q, k, v)):
        cols = pl.ds(j * HALF, HALF)
        for i, src in enumerate((xa, xb)):
            dst[pl.ds(i * ROWS, ROWS), :] = (
                jnp.dot(src[...], w[:, cols], preferred_element_type=jnp.float32) + bias[:, cols]
            ).astype(jnp.bfloat16)
    pair = 2 * HEAD
    lane = lax.broadcasted_iota(jnp.int32, (1, 256), 1)
    key_at = lax.broadcasted_iota(jnp.int32, (WIN, 1), 0)
    for wnd in range(2 * RECV):
        rows = pl.ds(wnd * WIN, WIN)
        live = key_at < MERGE * meta[4 + wnd]
        out = outa if wnd < RECV else outb
        tiles = [None] * (HALF // 128)
        for i in range(HALF // pair):
            lo = i * pair // 128 * 128
            off = i * pair - lo
            first = (lane >= off) & (lane < off + HEAD)
            second = (lane >= off + HEAD) & (lane < off + pair)
            cols = pl.ds(lo, 256)
            qw = q[rows, cols]
            q2 = jnp.concatenate(
                [
                    qw * first.astype(jnp.float32).astype(jnp.bfloat16),
                    qw * second.astype(jnp.float32).astype(jnp.bfloat16),
                ],
                axis=0,
            )
            s = lax.dot_general(k[rows, cols], q2, NT, preferred_element_type=jnp.float32)
            s = jnp.where(live, s * HEAD ** (-0.5), -1e30)
            e = jnp.exp(s - jnp.max(s, axis=0, keepdims=True))
            p = (e / jnp.sum(e, axis=0, keepdims=True)).astype(jnp.bfloat16)
            o = lax.dot_general(p, v[rows, cols], TN, preferred_element_type=jnp.float32)
            o = jnp.where(first, o[:WIN], jnp.where(second, o[WIN:], 0.0))
            for n in range(2):
                part = o[:, n * 128 : (n + 1) * 128]
                tile = lo // 128 + n
                tiles[tile] = part if tiles[tile] is None else tiles[tile] + part
        at = pl.ds(wnd % RECV * WIN, WIN)
        for n, tile in enumerate(tiles):
            out[at, pl.ds(n * 128, 128)] = tile.astype(jnp.bfloat16)


def merge_kernel(meta, atta, attb, wa, wb, placed, bias, gain, out, y):
    update = lax.dot_general(atta[...], wa[...], NT, preferred_element_type=jnp.float32)
    update += lax.dot_general(attb[...], wb[...], NT, preferred_element_type=jnp.float32)
    r = placed[...].astype(jnp.float32) + update + bias[...]
    ms = jnp.mean(r * r, axis=-1, keepdims=True)
    normed = r * lax.rsqrt(ms + EPS) * gain[...]
    for n in range(D // 128):
        y[n] = normed[:, n * 128 : (n + 1) * 128]
    tokens = WIN // MERGE
    at = lax.broadcasted_iota(jnp.int32, (RECV * tokens, 1), 0)
    limit = jnp.full((RECV * tokens, 1), meta[4], jnp.int32)
    for t in range(1, RECV):
        limit = jnp.where(at >= t * tokens, meta[4 + t] + t * tokens, limit)
    live = at < limit
    for i in range(MERGE):
        for n in range(D // 128):
            part = y[n, pl.ds(i, RECV * tokens, stride=MERGE), :]
            out[:, pl.ds(i * D + n * 128, 128)] = jnp.where(live, part, 0.0).astype(jnp.bfloat16)


def vmem(n):
    return [pl.BlockSpec(memory_space=pltpu.VMEM)] * n


ANY = pl.BlockSpec(memory_space=pl.ANY)
SMALL = pltpu.CompilerParams(vmem_limit_bytes=4 * 1024 * 1024)
SMEM = pl.BlockSpec(memory_space=pltpu.SMEM)
PARAMS = pltpu.CompilerParams(vmem_limit_bytes=20 * 1024 * 1024)


def tables(route, groups, rank, x, yh):
    ranks = lax.axis_size("dp")
    who = jnp.stack([rank, rank ^ 1])
    slot = jnp.arange(SLOTS, dtype=jnp.int32)
    sender = jnp.where(slot < RECV, who[:, None], (who[:, None] - slot + RECV - 1) % ranks)
    hot = sender[:, :, None] == jnp.arange(ranks, dtype=jnp.int32)
    lane_route = jnp.transpose(route[:, 0], (1, 2, 0))
    lane_groups = jnp.transpose(groups[:, 0], (1, 0))
    there = jnp.sum(jnp.where(hot[:, :, None], lane_route, 0), axis=-1)
    count = jnp.sum(jnp.where(hot, lane_groups, 0), axis=-1)
    target = jnp.arange(RECV, dtype=jnp.int32)
    lands = (there[:, :, 0] == who[:, None])[:, :, None] & (there[:, :, 1][:, :, None] == target)
    src = jnp.sum(jnp.where(lands, slot[None, :, None], 0), axis=1)
    grp = jnp.sum(jnp.where(lands, count[:, :, None], 0), axis=1)
    even = [(-1, 0), (0, 1), (-1, 1)]
    odd = [(1, 0), (2, 0), (2, 1)]
    orders = [
        [((x + dx) % NX) * NYH + (yh + dy) % NYH for dx, dy in [(0, 0), *one, *two, (1, 1)]]
        for one, two in ((even, odd), (odd, even))
    ]
    shard = jnp.where(rank % NC == 0, jnp.stack(orders[0]), jnp.stack(orders[1]))
    return jnp.concatenate([src[0], grp[0], grp[1], shard]).astype(jnp.int32)


def on_device(patches, norm_gain, w_qkv, b_qkv, w_proj, b_proj, merge_gain, groups, route):
    rank = lax.axis_index("dp")
    lane = lax.axis_index("fsdp")
    core = rank % NC
    half = core * HALF

    def columns(at):
        return jnp.concatenate(
            [lax.dynamic_slice_in_dim(w_qkv, j * D + at, HALF, 1) for j in range(3)]
            + [lax.dynamic_slice_in_dim(jnp.transpose(w_proj), at, HALF, 1)],
            axis=1,
        )

    piece = jnp.concatenate(
        lax.optimization_barrier([columns(half), columns(HALF - half)]), axis=0
    )
    bias = jnp.concatenate(
        [lax.dynamic_slice_in_dim(b_qkv, j * D + half, HALF, 0) for j in range(3)]
    )
    def halves_of(*shards):
        return jnp.concatenate([value[value.shape[0] // 2 :] for value in shards], axis=0)

    got_b = send(piece, moves((0, 1), (2, 0)))
    near = rank // NC % 2 * PART
    part = jnp.concatenate(
        [lax.dynamic_slice_in_dim(piece, i * DEPTH + near, PART, 0) for i in range(NC)], axis=0
    )
    got_a = send(part, moves((1, 0), (-1, 0)))
    moved = [by_rank(patches[0, 0, RECV + m], m + 1) for m in range(SLOTS - RECV)]
    got_b, *moved[:2] = lax.optimization_barrier((got_b, *moved[:2]))
    got_c = send(got_b, moves((1, 0), (0, 1)))
    got_d = send(got_b, moves((-1, 0)))
    rest_a = send(got_a, planes())
    early = send(halves_of(got_a, rest_a, got_b), other_core())

    meta = tables(route, groups, rank, lane // NYH, lane % NYH)

    placed, normed = pl.pallas_call(
        place_kernel,
        out_shape=[jax.ShapeDtypeStruct((ROWS, D), jnp.bfloat16)] * 2,
        in_specs=[SMEM] + [ANY] * 4 + vmem(1),
        out_specs=vmem(2),
        scratch_shapes=[pltpu.SemaphoreType.DMA((RECV,))],
        compiler_params=SMALL,
    )(meta, patches, *moved, norm_gain.reshape(1, D))
    normed_other = send(normed, other_core())
    late, normed_other = lax.optimization_barrier((halves_of(got_c, got_d), normed_other))
    late = send(late, other_core())

    w, w_mine = pl.pallas_call(
        gather_kernel,
        out_shape=[
            jax.ShapeDtypeStruct((D, 3 * HALF), jnp.bfloat16),
            jax.ShapeDtypeStruct((D, HALF), jnp.bfloat16),
        ],
        in_specs=[SMEM] + [ANY] * 9,
        out_specs=vmem(2),
        scratch_shapes=[pltpu.SemaphoreType.DMA((SHARDS + 2, 2))],
        compiler_params=PARAMS,
    )(meta, piece, got_a, got_b, got_c, got_d, rest_a, early, late, normed_other)
    w_other = send(w_mine, other_core())

    att, att_theirs = pl.pallas_call(
        attend_kernel,
        out_shape=[jax.ShapeDtypeStruct((ROWS, HALF), jnp.bfloat16)] * 2,
        in_specs=[SMEM] + vmem(4),
        out_specs=vmem(2),
        scratch_shapes=[pltpu.VMEM((2 * ROWS, HALF), jnp.bfloat16)] * 3,
        compiler_params=PARAMS,
    )(meta, normed, normed_other, bias.reshape(1, 3 * HALF), w)
    att_other = send(att_theirs, other_core())

    merged = pl.pallas_call(
        merge_kernel,
        out_shape=jax.ShapeDtypeStruct((ROWS // MERGE, MERGE * D), jnp.bfloat16),
        in_specs=[SMEM] + vmem(7),
        out_specs=vmem(1)[0],
        scratch_shapes=[pltpu.VMEM((D // 128, ROWS, 128), jnp.float32)],
        compiler_params=PARAMS,
    )(
        meta, att, att_other, w_mine, w_other, placed,
        b_proj.reshape(1, D), merge_gain.reshape(1, D),
    )
    return merged.reshape(1, 1, RECV, WIN // MERGE, MERGE * D)


def solution(mesh):
    return jax.shard_map(
        on_device,
        mesh=mesh,
        in_specs=(
            P("dp", "fsdp", None, None, None),
            P(),
            P("fsdp", None),
            P(),
            P(None, "fsdp"),
            P(),
            P(),
            P(None, "fsdp", None),
            P(None, "fsdp", None, None),
        ),
        out_specs=P("dp", "fsdp", None, None, None),
        check_vma=False,
    )
```

```python
import jax
import jax.numpy as jnp
from jax import lax
from jax.experimental import pallas as pl
from jax.experimental.pallas import tpu as pltpu
from jax.sharding import PartitionSpec as P

HEADS = 16
MERGE = 4
RECV = 4
SLOTS = 7
WIN = 64
D = 1280
HALF = D // 2
HEAD = D // HEADS
SHARDS = 8
DEPTH = D // SHARDS
PART = DEPTH // 2
ROWS = RECV * WIN
NX, NYH, NYL, NZ, NC = 4, 2, 2, 16, 2
AXES = ("dp", "fsdp")
EPS = 1e-06

NT = (((1,), (1,)), ((), ()))
TN = (((0,), (0,)), ((), ()))


def flat(x, yh, yl, z, c):
    return (((yl % NYL) * NZ + z % NZ) * NC + c) * SHARDS + (x % NX) * NYH + yh % NYH


def perm(move):
    places = [
        (x, yh, yl, z, c)
        for x in range(NX)
        for yh in range(NYH)
        for yl in range(NYL)
        for z in range(NZ)
        for c in range(NC)
    ]
    return [(flat(*p), flat(*move(*p))) for p in places]


def moves(even, odd=None):
    def move(x, yh, yl, z, c):
        dx, across = odd if c else even
        return x + dx, yh ^ across, yl ^ across, z, c

    pairs = perm(lambda *p: move(*p) if odd or p[-1] == 0 else p)
    return pairs if odd else [p for p in pairs if p[0] != p[1]]


def planes():
    return perm(lambda x, yh, yl, z, c: (x, yh, yl, z - 1 if c else z + 1, c))


def other_core():
    return perm(lambda x, yh, yl, z, c: (x, yh, yl, z, 1 - c))


def send(value, pairs):
    return lax.ppermute(value, AXES, pairs)


def by_rank(value, by):
    devices = lax.axis_size("dp")
    return lax.ppermute(value, "dp", [(i, (i + by) % devices) for i in range(devices)])


def place_kernel(meta, own, in0, in1, in2, gain, placed, normed, sems):
    for t in range(RECV):
        rows = placed.at[pl.ds(t * WIN, WIN), :]
        kept = own.at[0, 0, t]
        for at, ref in enumerate((kept, in0, in1, in2)):
            here = meta[t] < RECV if at == 0 else meta[t] == RECV - 1 + at

            @pl.when(here)
            def _(ref=ref, rows=rows, t=t):
                pltpu.make_async_copy(ref, rows, sems.at[t]).start()

    for t in range(RECV):
        rows = pl.ds(t * WIN, WIN)
        pltpu.make_async_copy(own.at[0, 0, t], placed.at[rows, :], sems.at[t]).wait()
        x = placed[rows, :].astype(jnp.float32)
        ms = jnp.mean(x * x, axis=-1, keepdims=True)
        normed[rows, :] = (x * lax.rsqrt(ms + EPS) * gain[...]).astype(jnp.bfloat16)


def halves_kernel(*refs):
    sources, out, sems = refs[:-2], refs[-2], refs[-1]
    copies, at = [], 0
    for i, ref in enumerate(sources):
        rows = ref.shape[0] // 2
        copies.append(
            pltpu.make_async_copy(
                ref.at[pl.ds(rows, rows), :], out.at[pl.ds(at, rows), :], sems.at[i]
            )
        )
        at += rows
    for copy in copies:
        copy.start()
    for copy in copies:
        copy.wait()


def gather_kernel(meta, own, a, b, c, d, rest_a, early, late, _, w, wo, sems):
    core = lax.rem(lax.axis_index("dp"), NC)
    near = lax.rem(lax.div(lax.axis_index("dp"), NC), 2) * PART
    away = PART - near
    sources = [
        (0, own, 0, DEPTH, 0),
        (1, a, 0, PART, near),
        (1, rest_a, 0, PART, away),
        (2, b, 0, DEPTH, 0),
        (3, c, 0, DEPTH, 0),
        (4, early, 0, PART, near),
        (4, early, PART, PART, away),
        (5, early, DEPTH, DEPTH, 0),
        (6, late, 0, DEPTH, 0),
    ]
    last = len(sources)

    def copies(i, shard, ref, row, rows, to):
        at = pl.multiple_of(meta[12 + shard] * DEPTH + to, PART)
        return [
            pltpu.make_async_copy(
                ref.at[pl.ds(row, rows), pl.ds(j * 3 * HALF, (3 - 2 * j) * HALF)],
                dst.at[pl.ds(at, rows), :],
                sems.at[i, j],
            )
            for j, dst in enumerate((w, wo))
        ]

    for i, source in enumerate(sources):
        for copy in copies(i, *source):
            copy.start()

    @pl.when(core == 0)
    def _():
        for copy in copies(last, SHARDS - 1, d, 0, DEPTH, 0):
            copy.start()

    @pl.when(core != 0)
    def _():
        for copy in copies(last, SHARDS - 1, late, DEPTH, DEPTH, 0):
            copy.start()

    for i, source in enumerate((*sources, (SHARDS - 1, late, DEPTH, DEPTH, 0))):
        for copy in copies(i, *source):
            copy.wait()


def attend_kernel(meta, xa, xb, bias, w, outa, outb, q, k, v):
    for j, dst in enumerate((q, k, v)):
        cols = pl.ds(j * HALF, HALF)
        for i, src in enumerate((xa, xb)):
            dst[pl.ds(i * ROWS, ROWS), :] = (
                jnp.dot(src[...], w[:, cols], preferred_element_type=jnp.float32) + bias[:, cols]
            ).astype(jnp.bfloat16)
    pair = 2 * HEAD
    lane = lax.broadcasted_iota(jnp.int32, (1, 256), 1)
    key_at = lax.broadcasted_iota(jnp.int32, (WIN, 1), 0)
    for wnd in range(2 * RECV):
        rows = pl.ds(wnd * WIN, WIN)
        live = key_at < MERGE * meta[4 + wnd]
        out = outa if wnd < RECV else outb
        tiles = [None] * (HALF // 128)
        for i in range(HALF // pair):
            lo = i * pair // 128 * 128
            off = i * pair - lo
            first = (lane >= off) & (lane < off + HEAD)
            second = (lane >= off + HEAD) & (lane < off + pair)
            cols = pl.ds(lo, 256)
            qw = q[rows, cols]
            q2 = jnp.concatenate(
                [
                    qw * first.astype(jnp.float32).astype(jnp.bfloat16),
                    qw * second.astype(jnp.float32).astype(jnp.bfloat16),
                ],
                axis=0,
            )
            s = lax.dot_general(k[rows, cols], q2, NT, preferred_element_type=jnp.float32)
            s = jnp.where(live, s * HEAD ** (-0.5), -1e30)
            e = jnp.exp(s - jnp.max(s, axis=0, keepdims=True))
            p = (e / jnp.sum(e, axis=0, keepdims=True)).astype(jnp.bfloat16)
            o = lax.dot_general(p, v[rows, cols], TN, preferred_element_type=jnp.float32)
            o = jnp.where(first, o[:WIN], jnp.where(second, o[WIN:], 0.0))
            for n in range(2):
                part = o[:, n * 128 : (n + 1) * 128]
                tile = lo // 128 + n
                tiles[tile] = part if tiles[tile] is None else tiles[tile] + part
        at = pl.ds(wnd % RECV * WIN, WIN)
        for n, tile in enumerate(tiles):
            out[at, pl.ds(n * 128, 128)] = tile.astype(jnp.bfloat16)


def merge_kernel(meta, atta, attb, wa, wb, placed, bias, gain, out, y):
    update = lax.dot_general(atta[...], wa[...], NT, preferred_element_type=jnp.float32)
    update += lax.dot_general(attb[...], wb[...], NT, preferred_element_type=jnp.float32)
    r = placed[...].astype(jnp.float32) + update + bias[...]
    ms = jnp.mean(r * r, axis=-1, keepdims=True)
    normed = r * lax.rsqrt(ms + EPS) * gain[...]
    for n in range(D // 128):
        y[n] = normed[:, n * 128 : (n + 1) * 128]
    tokens = WIN // MERGE
    at = lax.broadcasted_iota(jnp.int32, (RECV * tokens, 1), 0)
    limit = jnp.full((RECV * tokens, 1), meta[4], jnp.int32)
    for t in range(1, RECV):
        limit = jnp.where(at >= t * tokens, meta[4 + t] + t * tokens, limit)
    live = at < limit
    for i in range(MERGE):
        for n in range(D // 128):
            part = y[n, pl.ds(i, RECV * tokens, stride=MERGE), :]
            out[:, pl.ds(i * D + n * 128, 128)] = jnp.where(live, part, 0.0).astype(jnp.bfloat16)


COST = 2 * 10**10


def vmem(n):
    return [pl.BlockSpec(memory_space=pltpu.VMEM)] * n


ANY = pl.BlockSpec(memory_space=pl.ANY)
SMALL = pltpu.CompilerParams(vmem_limit_bytes=4 * 1024 * 1024)
SMEM = pl.BlockSpec(memory_space=pltpu.SMEM)
PARAMS = pltpu.CompilerParams(vmem_limit_bytes=20 * 1024 * 1024)


def gather_halves(*shards):
    return pl.pallas_call(
        halves_kernel,
        out_shape=jax.ShapeDtypeStruct((NC * DEPTH, 4 * HALF), jnp.bfloat16),
        in_specs=[ANY] * len(shards),
        out_specs=vmem(1)[0],
        scratch_shapes=[pltpu.SemaphoreType.DMA((len(shards),))],
        cost_estimate=pl.CostEstimate(
            flops=COST, bytes_accessed=4 * DEPTH * D, transcendentals=0
        ),
        compiler_params=SMALL,
    )(*shards)


def tables(route, groups, rank, x, yh):
    ranks = lax.axis_size("dp")
    who = jnp.stack([rank, rank ^ 1])
    slot = jnp.arange(SLOTS, dtype=jnp.int32)
    sender = jnp.where(slot < RECV, who[:, None], (who[:, None] - slot + RECV - 1) % ranks)
    hot = sender[:, :, None] == jnp.arange(ranks, dtype=jnp.int32)
    lane_route = jnp.transpose(route[:, 0], (1, 2, 0))
    lane_groups = jnp.transpose(groups[:, 0], (1, 0))
    there = jnp.sum(jnp.where(hot[:, :, None], lane_route, 0), axis=-1)
    count = jnp.sum(jnp.where(hot, lane_groups, 0), axis=-1)
    target = jnp.arange(RECV, dtype=jnp.int32)
    lands = (there[:, :, 0] == who[:, None])[:, :, None] & (there[:, :, 1][:, :, None] == target)
    src = jnp.sum(jnp.where(lands, slot[None, :, None], 0), axis=1)
    grp = jnp.sum(jnp.where(lands, count[:, :, None], 0), axis=1)
    even = [(-1, 0), (0, 1), (-1, 1)]
    odd = [(1, 0), (2, 0), (2, 1)]
    orders = [
        [((x + dx) % NX) * NYH + (yh + dy) % NYH for dx, dy in [(0, 0), *one, *two, (1, 1)]]
        for one, two in ((even, odd), (odd, even))
    ]
    shard = jnp.where(rank % NC == 0, jnp.stack(orders[0]), jnp.stack(orders[1]))
    return jnp.concatenate([src[0], grp[0], grp[1], shard]).astype(jnp.int32)


def on_device(patches, norm_gain, w_qkv, b_qkv, w_proj, b_proj, merge_gain, groups, route):
    rank = lax.axis_index("dp")
    lane = lax.axis_index("fsdp")
    core = rank % NC
    half = core * HALF

    def columns(at):
        return jnp.concatenate(
            [lax.dynamic_slice_in_dim(w_qkv, j * D + at, HALF, 1) for j in range(3)]
            + [lax.dynamic_slice_in_dim(jnp.transpose(w_proj), at, HALF, 1)],
            axis=1,
        )

    piece = jnp.concatenate(
        lax.optimization_barrier([columns(half), columns(HALF - half)]), axis=0
    )
    bias = jnp.concatenate(
        [lax.dynamic_slice_in_dim(b_qkv, j * D + half, HALF, 0) for j in range(3)]
    )
    got_b = send(piece, moves((0, 1), (2, 0)))
    near = rank // NC % 2 * PART
    part = jnp.concatenate(
        [lax.dynamic_slice_in_dim(piece, i * DEPTH + near, PART, 0) for i in range(NC)], axis=0
    )
    got_a = send(part, moves((1, 0), (-1, 0)))
    moved = [by_rank(patches[0, 0, RECV + m], m + 1) for m in range(SLOTS - RECV)]
    got_b, *moved[:2] = lax.optimization_barrier((got_b, *moved[:2]))
    got_c = send(got_b, moves((1, 0), (0, 1)))
    got_d = send(got_b, moves((-1, 0)))
    rest_a = send(got_a, planes())
    early = send(gather_halves(got_a, rest_a, got_b), other_core())

    meta = tables(route, groups, rank, lane // NYH, lane % NYH)

    placed, normed = pl.pallas_call(
        place_kernel,
        out_shape=[jax.ShapeDtypeStruct((ROWS, D), jnp.bfloat16)] * 2,
        in_specs=[SMEM] + [ANY] * 4 + vmem(1),
        out_specs=vmem(2),
        scratch_shapes=[pltpu.SemaphoreType.DMA((RECV,))],
        compiler_params=SMALL,
    )(meta, patches, *moved, norm_gain.reshape(1, D))
    normed_other = send(normed, other_core())
    late, normed_other = lax.optimization_barrier((gather_halves(got_c, got_d), normed_other))
    late = send(late, other_core())

    w, w_mine = pl.pallas_call(
        gather_kernel,
        out_shape=[
            jax.ShapeDtypeStruct((D, 3 * HALF), jnp.bfloat16),
            jax.ShapeDtypeStruct((D, HALF), jnp.bfloat16),
        ],
        in_specs=[SMEM] + [ANY] * 9,
        out_specs=vmem(2),
        scratch_shapes=[pltpu.SemaphoreType.DMA((SHARDS + 2, 2))],
        compiler_params=PARAMS,
    )(meta, piece, got_a, got_b, got_c, got_d, rest_a, early, late, normed_other)
    w_other = send(w_mine, other_core())

    att, att_theirs = pl.pallas_call(
        attend_kernel,
        out_shape=[jax.ShapeDtypeStruct((ROWS, HALF), jnp.bfloat16)] * 2,
        in_specs=[SMEM] + vmem(4),
        out_specs=vmem(2),
        scratch_shapes=[pltpu.VMEM((2 * ROWS, HALF), jnp.bfloat16)] * 3,
        compiler_params=PARAMS,
    )(meta, normed, normed_other, bias.reshape(1, 3 * HALF), w)
    att_other = send(att_theirs, other_core())

    merged = pl.pallas_call(
        merge_kernel,
        out_shape=jax.ShapeDtypeStruct((ROWS // MERGE, MERGE * D), jnp.bfloat16),
        in_specs=[SMEM] + vmem(7),
        out_specs=vmem(1)[0],
        scratch_shapes=[pltpu.VMEM((D // 128, ROWS, 128), jnp.float32)],
        compiler_params=PARAMS,
    )(
        meta, att, att_other, w_mine, w_other, placed,
        b_proj.reshape(1, D), merge_gain.reshape(1, D),
    )
    return merged.reshape(1, 1, RECV, WIN // MERGE, MERGE * D)


def solution(mesh):
    return jax.shard_map(
        on_device,
        mesh=mesh,
        in_specs=(
            P("dp", "fsdp", None, None, None),
            P(),
            P("fsdp", None),
            P(),
            P(None, "fsdp"),
            P(),
            P(),
            P(None, "fsdp", None),
            P(None, "fsdp", None, None),
        ),
        out_specs=P("dp", "fsdp", None, None, None),
        check_vma=False,
    )
```

```python
import jax
import jax.numpy as jnp
from jax import lax
from jax.experimental import pallas as pl
from jax.experimental.pallas import tpu as pltpu
from jax.sharding import PartitionSpec as P

HEADS = 16
MERGE = 4
RECV = 4
SLOTS = 7
WIN = 64
D = 1280
HALF = D // 2
HEAD = D // HEADS
SHARDS = 8
DEPTH = D // SHARDS
PART = DEPTH // 2
ROWS = RECV * WIN
NX, NYH, NYL, NZ, NC = 4, 2, 2, 16, 2
AXES = ("dp", "fsdp")
EPS = 1e-06

NT = (((1,), (1,)), ((), ()))
TN = (((0,), (0,)), ((), ()))


def flat(x, yh, yl, z, c):
    return (((yl % NYL) * NZ + z % NZ) * NC + c) * SHARDS + (x % NX) * NYH + yh % NYH


def perm(move):
    places = [
        (x, yh, yl, z, c)
        for x in range(NX)
        for yh in range(NYH)
        for yl in range(NYL)
        for z in range(NZ)
        for c in range(NC)
    ]
    return [(flat(*p), flat(*move(*p))) for p in places]


def moves(even, odd=None):
    def move(x, yh, yl, z, c):
        dx, across = odd if c else even
        return x + dx, yh ^ across, yl ^ across, z, c

    pairs = perm(lambda *p: move(*p) if odd or p[-1] == 0 else p)
    return pairs if odd else [p for p in pairs if p[0] != p[1]]


def planes():
    return perm(lambda x, yh, yl, z, c: (x, yh, yl, z - 1, c))


def other_core():
    return perm(lambda x, yh, yl, z, c: (x, yh, yl, z, 1 - c))


def send(value, pairs):
    return lax.ppermute(value, AXES, pairs)


def by_rank(value, by):
    devices = lax.axis_size("dp")
    return lax.ppermute(value, "dp", [(i, (i + by) % devices) for i in range(devices)])


def place_kernel(meta, own, in0, in1, in2, gain, placed, normed, sems):
    for t in range(RECV):
        rows = placed.at[pl.ds(t * WIN, WIN), :]
        kept = own.at[0, 0, t]
        for at, ref in enumerate((kept, in0, in1, in2)):
            here = meta[t] < RECV if at == 0 else meta[t] == RECV - 1 + at

            @pl.when(here)
            def _(ref=ref, rows=rows, t=t):
                pltpu.make_async_copy(ref, rows, sems.at[t]).start()

    for t in range(RECV):
        rows = pl.ds(t * WIN, WIN)
        pltpu.make_async_copy(own.at[0, 0, t], placed.at[rows, :], sems.at[t]).wait()
        x = placed[rows, :].astype(jnp.float32)
        ms = jnp.mean(x * x, axis=-1, keepdims=True)
        normed[rows, :] = (x * lax.rsqrt(ms + EPS) * gain[...]).astype(jnp.bfloat16)


def halves_kernel(*refs):
    sources, out, sems = refs[:-2], refs[-2], refs[-1]
    copies, at = [], 0
    for i, ref in enumerate(sources):
        rows = ref.shape[0] // 2
        copies.append(
            pltpu.make_async_copy(
                ref.at[pl.ds(rows, rows), :], out.at[pl.ds(at, rows), :], sems.at[i]
            )
        )
        at += rows
    for copy in copies:
        copy.start()
    for copy in copies:
        copy.wait()


def gather_kernel(meta, own, a, b, c, d, rest_a, early, late, _, w, wo, sems):
    core = lax.rem(lax.axis_index("dp"), NC)
    near = lax.rem(lax.div(lax.axis_index("dp"), NC), 2) * PART
    away = PART - near
    sources = [
        (0, own, 0, DEPTH, 0),
        (1, a, 0, PART, near),
        (1, rest_a, 0, PART, away),
        (2, b, 0, DEPTH, 0),
        (3, c, 0, DEPTH, 0),
        (4, early, 0, PART, near),
        (4, early, PART, PART, away),
        (5, early, DEPTH, DEPTH, 0),
        (6, late, 0, DEPTH, 0),
    ]
    last = len(sources)

    def copies(i, shard, ref, row, rows, to):
        at = pl.multiple_of(meta[12 + shard] * DEPTH + to, PART)
        return [
            pltpu.make_async_copy(
                ref.at[pl.ds(row, rows), pl.ds(j * 3 * HALF, (3 - 2 * j) * HALF)],
                dst.at[pl.ds(at, rows), :],
                sems.at[i, j],
            )
            for j, dst in enumerate((w, wo))
        ]

    for i, source in enumerate(sources):
        for copy in copies(i, *source):
            copy.start()

    @pl.when(core == 0)
    def _():
        for copy in copies(last, SHARDS - 1, d, 0, DEPTH, 0):
            copy.start()

    @pl.when(core != 0)
    def _():
        for copy in copies(last, SHARDS - 1, late, DEPTH, DEPTH, 0):
            copy.start()

    for i, source in enumerate((*sources, (SHARDS - 1, late, DEPTH, DEPTH, 0))):
        for copy in copies(i, *source):
            copy.wait()


def attend_kernel(meta, xa, xb, bias, w, outa, outb, q, k, v):
    for j, dst in enumerate((q, k, v)):
        cols = pl.ds(j * HALF, HALF)
        for i, src in enumerate((xa, xb)):
            dst[pl.ds(i * ROWS, ROWS), :] = (
                jnp.dot(src[...], w[:, cols], preferred_element_type=jnp.float32) + bias[:, cols]
            ).astype(jnp.bfloat16)
    pair = 2 * HEAD
    lane = lax.broadcasted_iota(jnp.int32, (1, 256), 1)
    key_at = lax.broadcasted_iota(jnp.int32, (WIN, 1), 0)
    for wnd in range(2 * RECV):
        rows = pl.ds(wnd * WIN, WIN)
        live = key_at < MERGE * meta[4 + wnd]
        out = outa if wnd < RECV else outb
        tiles = [None] * (HALF // 128)
        for i in range(HALF // pair):
            lo = i * pair // 128 * 128
            off = i * pair - lo
            first = (lane >= off) & (lane < off + HEAD)
            second = (lane >= off + HEAD) & (lane < off + pair)
            cols = pl.ds(lo, 256)
            qw = q[rows, cols]
            q2 = jnp.concatenate(
                [
                    qw * first.astype(jnp.float32).astype(jnp.bfloat16),
                    qw * second.astype(jnp.float32).astype(jnp.bfloat16),
                ],
                axis=0,
            )
            s = lax.dot_general(k[rows, cols], q2, NT, preferred_element_type=jnp.float32)
            s = jnp.where(live, s * HEAD ** (-0.5), -1e30)
            e = jnp.exp(s - jnp.max(s, axis=0, keepdims=True))
            p = (e / jnp.sum(e, axis=0, keepdims=True)).astype(jnp.bfloat16)
            o = lax.dot_general(p, v[rows, cols], TN, preferred_element_type=jnp.float32)
            o = jnp.where(first, o[:WIN], jnp.where(second, o[WIN:], 0.0))
            for n in range(2):
                part = o[:, n * 128 : (n + 1) * 128]
                tile = lo // 128 + n
                tiles[tile] = part if tiles[tile] is None else tiles[tile] + part
        at = pl.ds(wnd % RECV * WIN, WIN)
        for n, tile in enumerate(tiles):
            out[at, pl.ds(n * 128, 128)] = tile.astype(jnp.bfloat16)


def merge_kernel(meta, atta, attb, wa, wb, placed, bias, gain, out, y):
    update = lax.dot_general(atta[...], wa[...], NT, preferred_element_type=jnp.float32)
    update += lax.dot_general(attb[...], wb[...], NT, preferred_element_type=jnp.float32)
    r = placed[...].astype(jnp.float32) + update + bias[...]
    ms = jnp.mean(r * r, axis=-1, keepdims=True)
    normed = r * lax.rsqrt(ms + EPS) * gain[...]
    for n in range(D // 128):
        y[n] = normed[:, n * 128 : (n + 1) * 128]
    tokens = WIN // MERGE
    at = lax.broadcasted_iota(jnp.int32, (RECV * tokens, 1), 0)
    limit = jnp.full((RECV * tokens, 1), meta[4], jnp.int32)
    for t in range(1, RECV):
        limit = jnp.where(at >= t * tokens, meta[4 + t] + t * tokens, limit)
    live = at < limit
    for i in range(MERGE):
        for n in range(D // 128):
            part = y[n, pl.ds(i, RECV * tokens, stride=MERGE), :]
            out[:, pl.ds(i * D + n * 128, 128)] = jnp.where(live, part, 0.0).astype(jnp.bfloat16)


COST = 2 * 10**10


def vmem(n):
    return [pl.BlockSpec(memory_space=pltpu.VMEM)] * n


ANY = pl.BlockSpec(memory_space=pl.ANY)
SMALL = pltpu.CompilerParams(vmem_limit_bytes=4 * 1024 * 1024)
SMEM = pl.BlockSpec(memory_space=pltpu.SMEM)
PARAMS = pltpu.CompilerParams(vmem_limit_bytes=20 * 1024 * 1024)


def gather_halves(*shards):
    return pl.pallas_call(
        halves_kernel,
        out_shape=jax.ShapeDtypeStruct((NC * DEPTH, 4 * HALF), jnp.bfloat16),
        in_specs=[ANY] * len(shards),
        out_specs=vmem(1)[0],
        scratch_shapes=[pltpu.SemaphoreType.DMA((len(shards),))],
        cost_estimate=pl.CostEstimate(
            flops=COST, bytes_accessed=4 * DEPTH * D, transcendentals=0
        ),
        compiler_params=SMALL,
    )(*shards)


def tables(route, groups, rank, x, yh):
    ranks = lax.axis_size("dp")
    who = jnp.stack([rank, rank ^ 1])
    slot = jnp.arange(SLOTS, dtype=jnp.int32)
    sender = jnp.where(slot < RECV, who[:, None], (who[:, None] - slot + RECV - 1) % ranks)
    hot = sender[:, :, None] == jnp.arange(ranks, dtype=jnp.int32)
    lane_route = jnp.transpose(route[:, 0], (1, 2, 0))
    lane_groups = jnp.transpose(groups[:, 0], (1, 0))
    there = jnp.sum(jnp.where(hot[:, :, None], lane_route, 0), axis=-1)
    count = jnp.sum(jnp.where(hot, lane_groups, 0), axis=-1)
    target = jnp.arange(RECV, dtype=jnp.int32)
    lands = (there[:, :, 0] == who[:, None])[:, :, None] & (there[:, :, 1][:, :, None] == target)
    src = jnp.sum(jnp.where(lands, slot[None, :, None], 0), axis=1)
    grp = jnp.sum(jnp.where(lands, count[:, :, None], 0), axis=1)
    even = [(-1, 0), (0, 1), (-1, 1)]
    odd = [(1, 0), (2, 0), (2, 1)]
    orders = [
        [((x + dx) % NX) * NYH + (yh + dy) % NYH for dx, dy in [(0, 0), *one, *two, (1, 1)]]
        for one, two in ((even, odd), (odd, even))
    ]
    shard = jnp.where(rank % NC == 0, jnp.stack(orders[0]), jnp.stack(orders[1]))
    return jnp.concatenate([src[0], grp[0], grp[1], shard]).astype(jnp.int32)


def on_device(patches, norm_gain, w_qkv, b_qkv, w_proj, b_proj, merge_gain, groups, route):
    rank = lax.axis_index("dp")
    lane = lax.axis_index("fsdp")
    core = rank % NC
    half = core * HALF

    def columns(at):
        return jnp.concatenate(
            [lax.dynamic_slice_in_dim(w_qkv, j * D + at, HALF, 1) for j in range(3)]
            + [lax.dynamic_slice_in_dim(jnp.transpose(w_proj), at, HALF, 1)],
            axis=1,
        )

    piece = jnp.concatenate(
        lax.optimization_barrier([columns(half), columns(HALF - half)]), axis=0
    )
    bias = jnp.concatenate(
        [lax.dynamic_slice_in_dim(b_qkv, j * D + half, HALF, 0) for j in range(3)]
    )
    got_b = send(piece, moves((0, 1), (2, 0)))
    near = rank // NC % 2 * PART
    part = jnp.concatenate(
        [lax.dynamic_slice_in_dim(piece, i * DEPTH + near, PART, 0) for i in range(NC)], axis=0
    )
    got_a = send(part, moves((1, 0), (-1, 0)))
    moved = [by_rank(patches[0, 0, RECV + m], m + 1) for m in range(SLOTS - RECV)]
    got_b, *moved[:2] = lax.optimization_barrier((got_b, *moved[:2]))
    got_c = send(got_b, moves((1, 0), (0, 1)))
    got_d = send(got_b, moves((-1, 0)))
    rest_a = send(got_a, planes())
    early = send(gather_halves(got_a, rest_a, got_b), other_core())

    meta = tables(route, groups, rank, lane // NYH, lane % NYH)

    placed, normed = pl.pallas_call(
        place_kernel,
        out_shape=[jax.ShapeDtypeStruct((ROWS, D), jnp.bfloat16)] * 2,
        in_specs=[SMEM] + [ANY] * 4 + vmem(1),
        out_specs=vmem(2),
        scratch_shapes=[pltpu.SemaphoreType.DMA((RECV,))],
        compiler_params=SMALL,
    )(meta, patches, *moved, norm_gain.reshape(1, D))
    normed_other = send(normed, other_core())
    late, normed_other = lax.optimization_barrier((gather_halves(got_c, got_d), normed_other))
    late = send(late, other_core())

    w, w_mine = pl.pallas_call(
        gather_kernel,
        out_shape=[
            jax.ShapeDtypeStruct((D, 3 * HALF), jnp.bfloat16),
            jax.ShapeDtypeStruct((D, HALF), jnp.bfloat16),
        ],
        in_specs=[SMEM] + [ANY] * 9,
        out_specs=vmem(2),
        scratch_shapes=[pltpu.SemaphoreType.DMA((SHARDS + 2, 2))],
        compiler_params=PARAMS,
    )(meta, piece, got_a, got_b, got_c, got_d, rest_a, early, late, normed_other)
    w_other = send(w_mine, other_core())

    att, att_theirs = pl.pallas_call(
        attend_kernel,
        out_shape=[jax.ShapeDtypeStruct((ROWS, HALF), jnp.bfloat16)] * 2,
        in_specs=[SMEM] + vmem(4),
        out_specs=vmem(2),
        scratch_shapes=[pltpu.VMEM((2 * ROWS, HALF), jnp.bfloat16)] * 3,
        compiler_params=PARAMS,
    )(meta, normed, normed_other, bias.reshape(1, 3 * HALF), w)
    att_other = send(att_theirs, other_core())

    merged = pl.pallas_call(
        merge_kernel,
        out_shape=jax.ShapeDtypeStruct((ROWS // MERGE, MERGE * D), jnp.bfloat16),
        in_specs=[SMEM] + vmem(7),
        out_specs=vmem(1)[0],
        scratch_shapes=[pltpu.VMEM((D // 128, ROWS, 128), jnp.float32)],
        compiler_params=PARAMS,
    )(
        meta, att, att_other, w_mine, w_other, placed,
        b_proj.reshape(1, D), merge_gain.reshape(1, D),
    )
    return merged.reshape(1, 1, RECV, WIN // MERGE, MERGE * D)


def solution(mesh):
    return jax.shard_map(
        on_device,
        mesh=mesh,
        in_specs=(
            P("dp", "fsdp", None, None, None),
            P(),
            P("fsdp", None),
            P(),
            P(None, "fsdp"),
            P(),
            P(),
            P(None, "fsdp", None),
            P(None, "fsdp", None, None),
        ),
        out_specs=P("dp", "fsdp", None, None, None),
        check_vma=False,
    )
```

```python
import jax
import jax.numpy as jnp
from jax import lax
from jax.experimental import pallas as pl
from jax.experimental.pallas import tpu as pltpu
from jax.sharding import PartitionSpec as P

HEADS = 16
MERGE = 4
RECV = 4
SLOTS = 7
WIN = 64
D = 1280
HALF = D // 2
HEAD = D // HEADS
SHARDS = 8
DEPTH = D // SHARDS
PART = DEPTH // 2
ROWS = RECV * WIN
NX, NYH, NYL, NZ, NC = 4, 2, 2, 16, 2
AXES = ("dp", "fsdp")
EPS = 1e-06

NT = (((1,), (1,)), ((), ()))
TN = (((0,), (0,)), ((), ()))


def flat(x, yh, yl, z, c):
    return (((yl % NYL) * NZ + z % NZ) * NC + c) * SHARDS + (x % NX) * NYH + yh % NYH


def perm(move):
    places = [
        (x, yh, yl, z, c)
        for x in range(NX)
        for yh in range(NYH)
        for yl in range(NYL)
        for z in range(NZ)
        for c in range(NC)
    ]
    return [(flat(*p), flat(*move(*p))) for p in places]


def moves(even, odd=None):
    def move(x, yh, yl, z, c):
        dx, across = odd if c else even
        return x + dx, yh ^ across, yl ^ across, z, c

    pairs = perm(lambda *p: move(*p) if odd or p[-1] == 0 else p)
    return pairs if odd else [p for p in pairs if p[0] != p[1]]


def planes():
    return perm(lambda x, yh, yl, z, c: (x, yh, yl, z ^ 1, c))


def other_core():
    return perm(lambda x, yh, yl, z, c: (x, yh, yl, z, 1 - c))


def send(value, pairs):
    return lax.ppermute(value, AXES, pairs)


def by_rank(value, by):
    devices = lax.axis_size("dp")
    return lax.ppermute(value, "dp", [(i, (i + by) % devices) for i in range(devices)])


def place_kernel(meta, own, in0, in1, in2, gain, placed, normed, sems):
    for t in range(RECV):
        rows = placed.at[pl.ds(t * WIN, WIN), :]
        kept = own.at[0, 0, t]
        for at, ref in enumerate((kept, in0, in1, in2)):
            here = meta[t] < RECV if at == 0 else meta[t] == RECV - 1 + at

            @pl.when(here)
            def _(ref=ref, rows=rows, t=t):
                pltpu.make_async_copy(ref, rows, sems.at[t]).start()

    for t in range(RECV):
        rows = pl.ds(t * WIN, WIN)
        pltpu.make_async_copy(own.at[0, 0, t], placed.at[rows, :], sems.at[t]).wait()
        x = placed[rows, :].astype(jnp.float32)
        ms = jnp.mean(x * x, axis=-1, keepdims=True)
        normed[rows, :] = (x * lax.rsqrt(ms + EPS) * gain[...]).astype(jnp.bfloat16)


def halves_kernel(*refs):
    sources, out, sems = refs[:-2], refs[-2], refs[-1]
    copies, at = [], 0
    for i, ref in enumerate(sources):
        rows = ref.shape[0] // 2
        copies.append(
            pltpu.make_async_copy(
                ref.at[pl.ds(rows, rows), :], out.at[pl.ds(at, rows), :], sems.at[i]
            )
        )
        at += rows
    for copy in copies:
        copy.start()
    for copy in copies:
        copy.wait()


def gather_kernel(meta, own, a, b, c, d, rest_a, early, late, _, w, wo, sems):
    core = lax.rem(lax.axis_index("dp"), NC)
    near = lax.rem(lax.div(lax.axis_index("dp"), NC), 2) * PART
    away = PART - near
    sources = [
        (0, own, 0, DEPTH, 0),
        (1, a, 0, PART, near),
        (1, rest_a, 0, PART, away),
        (2, b, 0, DEPTH, 0),
        (3, c, 0, DEPTH, 0),
        (4, early, 0, PART, near),
        (4, early, PART, PART, away),
        (5, early, DEPTH, DEPTH, 0),
        (6, late, 0, DEPTH, 0),
    ]
    last = len(sources)

    def copies(i, shard, ref, row, rows, to):
        at = pl.multiple_of(meta[12 + shard] * DEPTH + to, PART)
        return [
            pltpu.make_async_copy(
                ref.at[pl.ds(row, rows), pl.ds(j * 3 * HALF, (3 - 2 * j) * HALF)],
                dst.at[pl.ds(at, rows), :],
                sems.at[i, j],
            )
            for j, dst in enumerate((w, wo))
        ]

    for i, source in enumerate(sources):
        for copy in copies(i, *source):
            copy.start()

    @pl.when(core == 0)
    def _():
        for copy in copies(last, SHARDS - 1, d, 0, DEPTH, 0):
            copy.start()

    @pl.when(core != 0)
    def _():
        for copy in copies(last, SHARDS - 1, late, DEPTH, DEPTH, 0):
            copy.start()

    for i, source in enumerate((*sources, (SHARDS - 1, late, DEPTH, DEPTH, 0))):
        for copy in copies(i, *source):
            copy.wait()


def attend_kernel(meta, xa, xb, bias, w, outa, outb, q, k, v):
    for j, dst in enumerate((q, k, v)):
        cols = pl.ds(j * HALF, HALF)
        for i, src in enumerate((xa, xb)):
            dst[pl.ds(i * ROWS, ROWS), :] = (
                jnp.dot(src[...], w[:, cols], preferred_element_type=jnp.float32) + bias[:, cols]
            ).astype(jnp.bfloat16)
    pair = 2 * HEAD
    lane = lax.broadcasted_iota(jnp.int32, (1, 256), 1)
    key_at = lax.broadcasted_iota(jnp.int32, (WIN, 1), 0)
    for wnd in range(2 * RECV):
        rows = pl.ds(wnd * WIN, WIN)
        live = key_at < MERGE * meta[4 + wnd]
        out = outa if wnd < RECV else outb
        tiles = [None] * (HALF // 128)
        for i in range(HALF // pair):
            lo = i * pair // 128 * 128
            off = i * pair - lo
            first = (lane >= off) & (lane < off + HEAD)
            second = (lane >= off + HEAD) & (lane < off + pair)
            cols = pl.ds(lo, 256)
            qw = q[rows, cols]
            q2 = jnp.concatenate(
                [
                    qw * first.astype(jnp.float32).astype(jnp.bfloat16),
                    qw * second.astype(jnp.float32).astype(jnp.bfloat16),
                ],
                axis=0,
            )
            s = lax.dot_general(k[rows, cols], q2, NT, preferred_element_type=jnp.float32)
            s = jnp.where(live, s * HEAD ** (-0.5), -1e30)
            e = jnp.exp(s - jnp.max(s, axis=0, keepdims=True))
            p = (e / jnp.sum(e, axis=0, keepdims=True)).astype(jnp.bfloat16)
            o = lax.dot_general(p, v[rows, cols], TN, preferred_element_type=jnp.float32)
            o = jnp.where(first, o[:WIN], jnp.where(second, o[WIN:], 0.0))
            for n in range(2):
                part = o[:, n * 128 : (n + 1) * 128]
                tile = lo // 128 + n
                tiles[tile] = part if tiles[tile] is None else tiles[tile] + part
        at = pl.ds(wnd % RECV * WIN, WIN)
        for n, tile in enumerate(tiles):
            out[at, pl.ds(n * 128, 128)] = tile.astype(jnp.bfloat16)


def merge_kernel(meta, atta, attb, wa, wb, placed, bias, gain, out, y):
    update = lax.dot_general(atta[...], wa[...], NT, preferred_element_type=jnp.float32)
    update += lax.dot_general(attb[...], wb[...], NT, preferred_element_type=jnp.float32)
    r = placed[...].astype(jnp.float32) + update + bias[...]
    ms = jnp.mean(r * r, axis=-1, keepdims=True)
    normed = r * lax.rsqrt(ms + EPS) * gain[...]
    for n in range(D // 128):
        y[n] = normed[:, n * 128 : (n + 1) * 128]
    tokens = WIN // MERGE
    at = lax.broadcasted_iota(jnp.int32, (RECV * tokens, 1), 0)
    limit = jnp.full((RECV * tokens, 1), meta[4], jnp.int32)
    for t in range(1, RECV):
        limit = jnp.where(at >= t * tokens, meta[4 + t] + t * tokens, limit)
    live = at < limit
    for i in range(MERGE):
        for n in range(D // 128):
            part = y[n, pl.ds(i, RECV * tokens, stride=MERGE), :]
            out[:, pl.ds(i * D + n * 128, 128)] = jnp.where(live, part, 0.0).astype(jnp.bfloat16)


COST = 2 * 10**10


def vmem(n):
    return [pl.BlockSpec(memory_space=pltpu.VMEM)] * n


ANY = pl.BlockSpec(memory_space=pl.ANY)
SMALL = pltpu.CompilerParams(vmem_limit_bytes=4 * 1024 * 1024)
SMEM = pl.BlockSpec(memory_space=pltpu.SMEM)
PARAMS = pltpu.CompilerParams(vmem_limit_bytes=20 * 1024 * 1024)


def gather_halves(*shards):
    return pl.pallas_call(
        halves_kernel,
        out_shape=jax.ShapeDtypeStruct((NC * DEPTH, 4 * HALF), jnp.bfloat16),
        in_specs=[ANY] * len(shards),
        out_specs=vmem(1)[0],
        scratch_shapes=[pltpu.SemaphoreType.DMA((len(shards),))],
        cost_estimate=pl.CostEstimate(
            flops=COST, bytes_accessed=4 * DEPTH * D, transcendentals=0
        ),
        compiler_params=SMALL,
    )(*shards)


def tables(route, groups, rank, x, yh):
    ranks = lax.axis_size("dp")
    who = jnp.stack([rank, rank ^ 1])
    slot = jnp.arange(SLOTS, dtype=jnp.int32)
    sender = jnp.where(slot < RECV, who[:, None], (who[:, None] - slot + RECV - 1) % ranks)
    hot = sender[:, :, None] == jnp.arange(ranks, dtype=jnp.int32)
    lane_route = jnp.transpose(route[:, 0], (1, 2, 0))
    lane_groups = jnp.transpose(groups[:, 0], (1, 0))
    there = jnp.sum(jnp.where(hot[:, :, None], lane_route, 0), axis=-1)
    count = jnp.sum(jnp.where(hot, lane_groups, 0), axis=-1)
    target = jnp.arange(RECV, dtype=jnp.int32)
    lands = (there[:, :, 0] == who[:, None])[:, :, None] & (there[:, :, 1][:, :, None] == target)
    src = jnp.sum(jnp.where(lands, slot[None, :, None], 0), axis=1)
    grp = jnp.sum(jnp.where(lands, count[:, :, None], 0), axis=1)
    even = [(-1, 0), (0, 1), (-1, 1)]
    odd = [(1, 0), (2, 0), (2, 1)]
    orders = [
        [((x + dx) % NX) * NYH + (yh + dy) % NYH for dx, dy in [(0, 0), *one, *two, (1, 1)]]
        for one, two in ((even, odd), (odd, even))
    ]
    shard = jnp.where(rank % NC == 0, jnp.stack(orders[0]), jnp.stack(orders[1]))
    return jnp.concatenate([src[0], grp[0], grp[1], shard]).astype(jnp.int32)


def on_device(patches, norm_gain, w_qkv, b_qkv, w_proj, b_proj, merge_gain, groups, route):
    rank = lax.axis_index("dp")
    lane = lax.axis_index("fsdp")
    core = rank % NC
    half = core * HALF

    def columns(at):
        return jnp.concatenate(
            [lax.dynamic_slice_in_dim(w_qkv, j * D + at, HALF, 1) for j in range(3)]
            + [lax.dynamic_slice_in_dim(jnp.transpose(w_proj), at, HALF, 1)],
            axis=1,
        )

    piece = jnp.concatenate(
        lax.optimization_barrier([columns(half), columns(HALF - half)]), axis=0
    )
    bias = jnp.concatenate(
        [lax.dynamic_slice_in_dim(b_qkv, j * D + half, HALF, 0) for j in range(3)]
    )
    got_b = send(piece, moves((0, 1), (2, 0)))
    near = rank // NC % 2 * PART
    part = jnp.concatenate(
        [lax.dynamic_slice_in_dim(piece, i * DEPTH + near, PART, 0) for i in range(NC)], axis=0
    )
    got_a = send(part, moves((1, 0), (-1, 0)))
    moved = [by_rank(patches[0, 0, RECV + m], m + 1) for m in range(SLOTS - RECV)]
    got_b, *moved[:2] = lax.optimization_barrier((got_b, *moved[:2]))
    got_c = send(got_b, moves((1, 0), (0, 1)))
    got_d = send(got_b, moves((-1, 0)))
    rest_a = send(got_a, planes())
    early = send(gather_halves(got_a, rest_a, got_b), other_core())

    meta = tables(route, groups, rank, lane // NYH, lane % NYH)

    placed, normed = pl.pallas_call(
        place_kernel,
        out_shape=[jax.ShapeDtypeStruct((ROWS, D), jnp.bfloat16)] * 2,
        in_specs=[SMEM] + [ANY] * 4 + vmem(1),
        out_specs=vmem(2),
        scratch_shapes=[pltpu.SemaphoreType.DMA((RECV,))],
        compiler_params=SMALL,
    )(meta, patches, *moved, norm_gain.reshape(1, D))
    normed_other = send(normed, other_core())
    late, normed_other = lax.optimization_barrier((gather_halves(got_c, got_d), normed_other))
    late = send(late, other_core())

    w, w_mine = pl.pallas_call(
        gather_kernel,
        out_shape=[
            jax.ShapeDtypeStruct((D, 3 * HALF), jnp.bfloat16),
            jax.ShapeDtypeStruct((D, HALF), jnp.bfloat16),
        ],
        in_specs=[SMEM] + [ANY] * 9,
        out_specs=vmem(2),
        scratch_shapes=[pltpu.SemaphoreType.DMA((SHARDS + 2, 2))],
        compiler_params=PARAMS,
    )(meta, piece, got_a, got_b, got_c, got_d, rest_a, early, late, normed_other)
    w_other = send(w_mine, other_core())

    att, att_theirs = pl.pallas_call(
        attend_kernel,
        out_shape=[jax.ShapeDtypeStruct((ROWS, HALF), jnp.bfloat16)] * 2,
        in_specs=[SMEM] + vmem(4),
        out_specs=vmem(2),
        scratch_shapes=[pltpu.VMEM((2 * ROWS, HALF), jnp.bfloat16)] * 3,
        compiler_params=PARAMS,
    )(meta, normed, normed_other, bias.reshape(1, 3 * HALF), w)
    att_other = send(att_theirs, other_core())

    merged = pl.pallas_call(
        merge_kernel,
        out_shape=jax.ShapeDtypeStruct((ROWS // MERGE, MERGE * D), jnp.bfloat16),
        in_specs=[SMEM] + vmem(7),
        out_specs=vmem(1)[0],
        scratch_shapes=[pltpu.VMEM((D // 128, ROWS, 128), jnp.float32)],
        compiler_params=PARAMS,
    )(
        meta, att, att_other, w_mine, w_other, placed,
        b_proj.reshape(1, D), merge_gain.reshape(1, D),
    )
    return merged.reshape(1, 1, RECV, WIN // MERGE, MERGE * D)


def solution(mesh):
    return jax.shard_map(
        on_device,
        mesh=mesh,
        in_specs=(
            P("dp", "fsdp", None, None, None),
            P(),
            P("fsdp", None),
            P(),
            P(None, "fsdp"),
            P(),
            P(),
            P(None, "fsdp", None),
            P(None, "fsdp", None, None),
        ),
        out_specs=P("dp", "fsdp", None, None, None),
        check_vma=False,
    )
```

```python
import jax
import jax.numpy as jnp
from jax import lax
from jax.experimental import pallas as pl
from jax.experimental.pallas import tpu as pltpu
from jax.sharding import PartitionSpec as P

HEADS = 16
MERGE = 4
RECV = 4
SLOTS = 7
WIN = 64
D = 1280
HALF = D // 2
HEAD = D // HEADS
SHARDS = 8
DEPTH = D // SHARDS
PART = DEPTH // 2
ROWS = RECV * WIN
NX, NYH, NYL, NZ, NC = 4, 2, 2, 16, 2
AXES = ("dp", "fsdp")
EPS = 1e-06

NT = (((1,), (1,)), ((), ()))
TN = (((0,), (0,)), ((), ()))


def flat(x, yh, yl, z, c):
    return (((yl % NYL) * NZ + z % NZ) * NC + c) * SHARDS + (x % NX) * NYH + yh % NYH


def perm(move):
    places = [
        (x, yh, yl, z, c)
        for x in range(NX)
        for yh in range(NYH)
        for yl in range(NYL)
        for z in range(NZ)
        for c in range(NC)
    ]
    return [(flat(*p), flat(*move(*p))) for p in places]


def moves(even, odd=None):
    def move(x, yh, yl, z, c):
        dx, across = odd if c else even
        return x + dx, yh ^ across, yl ^ across, z, c

    pairs = perm(lambda *p: move(*p) if odd or p[-1] == 0 else p)
    return pairs if odd else [p for p in pairs if p[0] != p[1]]


def planes():
    return perm(lambda x, yh, yl, z, c: (x, yh, yl, z ^ 1, c))


def other_core():
    return perm(lambda x, yh, yl, z, c: (x, yh, yl, z, 1 - c))


def send(value, pairs):
    return lax.ppermute(value, AXES, pairs)


def by_rank(value, by):
    devices = lax.axis_size("dp")
    return lax.ppermute(value, "dp", [(i, (i + by) % devices) for i in range(devices)])


def place_kernel(meta, own, in0, in1, in2, gain, placed, normed, sems):
    for t in range(RECV):
        rows = placed.at[pl.ds(t * WIN, WIN), :]
        kept = own.at[0, 0, t]
        for at, ref in enumerate((kept, in0, in1, in2)):
            here = meta[t] < RECV if at == 0 else meta[t] == RECV - 1 + at

            @pl.when(here)
            def _(ref=ref, rows=rows, t=t):
                pltpu.make_async_copy(ref, rows, sems.at[t]).start()

    for t in range(RECV):
        rows = pl.ds(t * WIN, WIN)
        pltpu.make_async_copy(own.at[0, 0, t], placed.at[rows, :], sems.at[t]).wait()
        x = placed[rows, :].astype(jnp.float32)
        ms = jnp.mean(x * x, axis=-1, keepdims=True)
        normed[rows, :] = (x * lax.rsqrt(ms + EPS) * gain[...]).astype(jnp.bfloat16)


def halves_kernel(*refs):
    sources, out, sems = refs[:-2], refs[-2], refs[-1]
    copies, at = [], 0
    for i, ref in enumerate(sources):
        rows = ref.shape[0] // 2
        copies.append(
            pltpu.make_async_copy(
                ref.at[pl.ds(rows, rows), :], out.at[pl.ds(at, rows), :], sems.at[i]
            )
        )
        at += rows
    for copy in copies:
        copy.start()
    for copy in copies:
        copy.wait()


def gather_kernel(meta, own, a, b, c, d, rest_a, early, late, _, w, wo, sems):
    core = lax.rem(lax.axis_index("dp"), NC)
    near = lax.rem(lax.div(lax.axis_index("dp"), NC), 2) * PART
    away = PART - near
    sources = [
        (0, own, 0, DEPTH, 0),
        (1, a, 0, PART, near),
        (1, rest_a, 0, PART, away),
        (2, b, 0, DEPTH, 0),
        (3, c, 0, DEPTH, 0),
        (4, early, 0, PART, near),
        (4, early, PART, PART, away),
        (5, early, DEPTH, DEPTH, 0),
        (6, late, 0, DEPTH, 0),
    ]
    last = len(sources)

    def copies(i, shard, ref, row, rows, to):
        at = pl.multiple_of(meta[12 + shard] * DEPTH + to, PART)
        return [
            pltpu.make_async_copy(
                ref.at[pl.ds(row, rows), pl.ds(j * 3 * HALF, (3 - 2 * j) * HALF)],
                dst.at[pl.ds(at, rows), :],
                sems.at[i, j],
            )
            for j, dst in enumerate((w, wo))
        ]

    for i, source in enumerate(sources):
        for copy in copies(i, *source):
            copy.start()

    @pl.when(core == 0)
    def _():
        for copy in copies(last, SHARDS - 1, d, 0, DEPTH, 0):
            copy.start()

    @pl.when(core != 0)
    def _():
        for copy in copies(last, SHARDS - 1, late, DEPTH, DEPTH, 0):
            copy.start()

    for i, source in enumerate((*sources, (SHARDS - 1, late, DEPTH, DEPTH, 0))):
        for copy in copies(i, *source):
            copy.wait()


def attend_kernel(meta, xa, xb, bias, w, outa, outb, q, k, v):
    for j, dst in enumerate((q, k, v)):
        cols = pl.ds(j * HALF, HALF)
        for i, src in enumerate((xa, xb)):
            dst[pl.ds(i * ROWS, ROWS), :] = (
                jnp.dot(src[...], w[:, cols], preferred_element_type=jnp.float32) + bias[:, cols]
            ).astype(jnp.bfloat16)
    pair = 2 * HEAD
    lane = lax.broadcasted_iota(jnp.int32, (1, 256), 1)
    key_at = lax.broadcasted_iota(jnp.int32, (WIN, 1), 0)
    for wnd in range(2 * RECV):
        rows = pl.ds(wnd * WIN, WIN)
        live = key_at < MERGE * meta[4 + wnd]
        out = outa if wnd < RECV else outb
        tiles = [None] * (HALF // 128)
        for i in range(HALF // pair):
            lo = i * pair // 128 * 128
            off = i * pair - lo
            first = (lane >= off) & (lane < off + HEAD)
            second = (lane >= off + HEAD) & (lane < off + pair)
            cols = pl.ds(lo, 256)
            qw = q[rows, cols]
            q2 = jnp.concatenate(
                [
                    qw * first.astype(jnp.float32).astype(jnp.bfloat16),
                    qw * second.astype(jnp.float32).astype(jnp.bfloat16),
                ],
                axis=0,
            )
            s = lax.dot_general(k[rows, cols], q2, NT, preferred_element_type=jnp.float32)
            s = jnp.where(live, s * HEAD ** (-0.5), -1e30)
            e = jnp.exp(s - jnp.max(s, axis=0, keepdims=True))
            p = (e / jnp.sum(e, axis=0, keepdims=True)).astype(jnp.bfloat16)
            o = lax.dot_general(p, v[rows, cols], TN, preferred_element_type=jnp.float32)
            o = jnp.where(first, o[:WIN], jnp.where(second, o[WIN:], 0.0))
            for n in range(2):
                part = o[:, n * 128 : (n + 1) * 128]
                tile = lo // 128 + n
                tiles[tile] = part if tiles[tile] is None else tiles[tile] + part
        at = pl.ds(wnd % RECV * WIN, WIN)
        for n, tile in enumerate(tiles):
            out[at, pl.ds(n * 128, 128)] = tile.astype(jnp.bfloat16)


def merge_kernel(meta, atta, attb, wa, wb, placed, bias, gain, out, y):
    update = lax.dot_general(atta[...], wa[...], NT, preferred_element_type=jnp.float32)
    update += lax.dot_general(attb[...], wb[...], NT, preferred_element_type=jnp.float32)
    r = placed[...].astype(jnp.float32) + update + bias[...]
    ms = jnp.mean(r * r, axis=-1, keepdims=True)
    normed = r * lax.rsqrt(ms + EPS) * gain[...]
    for n in range(D // 128):
        y[n] = normed[:, n * 128 : (n + 1) * 128]
    tokens = WIN // MERGE
    at = lax.broadcasted_iota(jnp.int32, (RECV * tokens, 1), 0)
    limit = jnp.full((RECV * tokens, 1), meta[4], jnp.int32)
    for t in range(1, RECV):
        limit = jnp.where(at >= t * tokens, meta[4 + t] + t * tokens, limit)
    live = at < limit
    for i in range(MERGE):
        for n in range(D // 128):
            part = y[n, pl.ds(i, RECV * tokens, stride=MERGE), :]
            out[:, pl.ds(i * D + n * 128, 128)] = jnp.where(live, part, 0.0).astype(jnp.bfloat16)


COST = 2 * 10**10


def vmem(n):
    return [pl.BlockSpec(memory_space=pltpu.VMEM)] * n


ANY = pl.BlockSpec(memory_space=pl.ANY)
SMALL = pltpu.CompilerParams(vmem_limit_bytes=4 * 1024 * 1024)
SMEM = pl.BlockSpec(memory_space=pltpu.SMEM)
PARAMS = pltpu.CompilerParams(vmem_limit_bytes=20 * 1024 * 1024)


def gather_halves(*shards):
    return pl.pallas_call(
        halves_kernel,
        out_shape=jax.ShapeDtypeStruct((NC * DEPTH, 4 * HALF), jnp.bfloat16),
        in_specs=[ANY] * len(shards),
        out_specs=vmem(1)[0],
        scratch_shapes=[pltpu.SemaphoreType.DMA((len(shards),))],
        cost_estimate=pl.CostEstimate(
            flops=COST, bytes_accessed=4 * DEPTH * D, transcendentals=0
        ),
        compiler_params=SMALL,
    )(*shards)


def tables(route, groups, rank, x, yh):
    ranks = lax.axis_size("dp")
    who = jnp.stack([rank, rank ^ 1])
    slot = jnp.arange(SLOTS, dtype=jnp.int32)
    sender = jnp.where(slot < RECV, who[:, None], (who[:, None] - slot + RECV - 1) % ranks)
    hot = sender[:, :, None] == jnp.arange(ranks, dtype=jnp.int32)
    lane_route = jnp.transpose(route[:, 0], (1, 2, 0))
    lane_groups = jnp.transpose(groups[:, 0], (1, 0))
    there = jnp.sum(jnp.where(hot[:, :, None], lane_route, 0), axis=-1)
    count = jnp.sum(jnp.where(hot, lane_groups, 0), axis=-1)
    target = jnp.arange(RECV, dtype=jnp.int32)
    lands = (there[:, :, 0] == who[:, None])[:, :, None] & (there[:, :, 1][:, :, None] == target)
    src = jnp.sum(jnp.where(lands, slot[None, :, None], 0), axis=1)
    grp = jnp.sum(jnp.where(lands, count[:, :, None], 0), axis=1)
    even = [(-1, 0), (0, 1), (-1, 1)]
    odd = [(1, 0), (2, 0), (2, 1)]
    orders = [
        [((x + dx) % NX) * NYH + (yh + dy) % NYH for dx, dy in [(0, 0), *one, *two, (1, 1)]]
        for one, two in ((even, odd), (odd, even))
    ]
    shard = jnp.where(rank % NC == 0, jnp.stack(orders[0]), jnp.stack(orders[1]))
    return jnp.concatenate([src[0], grp[0], grp[1], shard]).astype(jnp.int32)


def on_device(patches, norm_gain, w_qkv, b_qkv, w_proj, b_proj, merge_gain, groups, route):
    rank = lax.axis_index("dp")
    lane = lax.axis_index("fsdp")
    core = rank % NC
    half = core * HALF

    def columns(at):
        return jnp.concatenate(
            [lax.dynamic_slice_in_dim(w_qkv, j * D + at, HALF, 1) for j in range(3)]
            + [lax.dynamic_slice_in_dim(jnp.transpose(w_proj), at, HALF, 1)],
            axis=1,
        )

    piece = jnp.concatenate(
        lax.optimization_barrier([columns(half), columns(HALF - half)]), axis=0
    )
    bias = jnp.concatenate(
        [lax.dynamic_slice_in_dim(b_qkv, j * D + half, HALF, 0) for j in range(3)]
    )
    got_b = send(piece, moves((0, 1), (2, 0)))
    near = rank // NC % 2 * PART
    part = jnp.concatenate(
        [lax.dynamic_slice_in_dim(piece, i * DEPTH + near, PART, 0) for i in range(NC)], axis=0
    )
    got_a = send(part, moves((1, 0), (-1, 0)))
    moved = [by_rank(patches[0, 0, RECV + m], m + 1) for m in range(SLOTS - RECV)]
    got_b, *moved[:2] = lax.optimization_barrier((got_b, *moved[:2]))
    got_c = send(got_b, moves((1, 0), (0, 1)))
    got_d = send(got_b, moves((-1, 0)))
    rest_a = send(got_a, planes())
    early = send(gather_halves(got_a, rest_a, got_b), other_core())

    meta = tables(route, groups, rank, lane // NYH, lane % NYH)

    placed, normed = pl.pallas_call(
        place_kernel,
        out_shape=[jax.ShapeDtypeStruct((ROWS, D), jnp.bfloat16)] * 2,
        in_specs=[SMEM] + [ANY] * 4 + vmem(1),
        out_specs=vmem(2),
        scratch_shapes=[pltpu.SemaphoreType.DMA((RECV,))],
        compiler_params=SMALL,
    )(meta, patches, *moved, norm_gain.reshape(1, D))
    normed_other = send(normed, other_core())
    late = gather_halves(got_c, got_d)
    late = send(late, other_core())

    w, w_mine = pl.pallas_call(
        gather_kernel,
        out_shape=[
            jax.ShapeDtypeStruct((D, 3 * HALF), jnp.bfloat16),
            jax.ShapeDtypeStruct((D, HALF), jnp.bfloat16),
        ],
        in_specs=[SMEM] + [ANY] * 9,
        out_specs=vmem(2),
        scratch_shapes=[pltpu.SemaphoreType.DMA((SHARDS + 2, 2))],
        compiler_params=PARAMS,
    )(meta, piece, got_a, got_b, got_c, got_d, rest_a, early, late, normed_other)
    w_other = send(w_mine, other_core())

    att, att_theirs = pl.pallas_call(
        attend_kernel,
        out_shape=[jax.ShapeDtypeStruct((ROWS, HALF), jnp.bfloat16)] * 2,
        in_specs=[SMEM] + vmem(4),
        out_specs=vmem(2),
        scratch_shapes=[pltpu.VMEM((2 * ROWS, HALF), jnp.bfloat16)] * 3,
        compiler_params=PARAMS,
    )(meta, normed, normed_other, bias.reshape(1, 3 * HALF), w)
    att_other = send(att_theirs, other_core())

    merged = pl.pallas_call(
        merge_kernel,
        out_shape=jax.ShapeDtypeStruct((ROWS // MERGE, MERGE * D), jnp.bfloat16),
        in_specs=[SMEM] + vmem(7),
        out_specs=vmem(1)[0],
        scratch_shapes=[pltpu.VMEM((D // 128, ROWS, 128), jnp.float32)],
        compiler_params=PARAMS,
    )(
        meta, att, att_other, w_mine, w_other, placed,
        b_proj.reshape(1, D), merge_gain.reshape(1, D),
    )
    return merged.reshape(1, 1, RECV, WIN // MERGE, MERGE * D)


def solution(mesh):
    return jax.shard_map(
        on_device,
        mesh=mesh,
        in_specs=(
            P("dp", "fsdp", None, None, None),
            P(),
            P("fsdp", None),
            P(),
            P(None, "fsdp"),
            P(),
            P(),
            P(None, "fsdp", None),
            P(None, "fsdp", None, None),
        ),
        out_specs=P("dp", "fsdp", None, None, None),
        check_vma=False,
    )
```
